32 devices in a mesh: seg: 8 (over y, x, core), tensor: 4 (over z).
Axes of the slice: x: 2, y: 2, z: 4, core: 2. Of those that a mesh axis runs over, the one named last changes fastest.
Arguments:
- tokens: bfloat16 [8704, 8192], P(('seg', 'tensor')), may hold values from -6 to 6
- memory_embed: bfloat16 [64, 8192], P('tensor'), may hold values from -6 to 6
- norm_gain: bfloat16 [8192], replicated, may hold values from 0.5 to 1.5
- w_query: bfloat16 [8192, 4096], P(None, 'tensor'), as said below
- w_key: bfloat16 [8192, 1024], P(None, 'tensor'), as said below
- value_weight: bfloat16 [8192, 1024], P(None, 'tensor'), may hold values from -0.0625 to 0.0625
- w_out: bfloat16 [4096, 8192], P('tensor'), may hold values from -0.09375 to 0.09375
- retain: float32 [8, 32], P('seg', 'tensor'), may hold values from 0.05 to 1
Outputs:
- output: bfloat16 [8704, 8192], P(('seg', 'tensor'))
The draws below stay inside these ranges and needn't reach their ends.
Inputs may be any that keep to these rules, and one draw needn't show every extreme that they name: `w_query`: entries lie within 6 / sqrt(8192) of zero. `w_key`: entries lie within 6 / sqrt(8192) of zero.
All inputs are finite; a program needn't handle non-finite values.
Results may differ from the reference program's by a relative error of at most 0.007.
Values may be sent and summed in bfloat16 or wider, within the bound.
No kernel may reach another device: no remote copies, remote signals or barrier semaphores. Data moves between devices by JAX's collectives and lax.ppermute only.
A program may use at most 192 MiB of HBM per device.

```python
import math
import jax
import jax.numpy as jnp
from jax import lax

MODEL_WIDTH = 8192
HQ = 32
KEY_VALUE_HEADS = 8
HEAD_SIZE = 128
MEM = 64
SEG = 1088
TOKENS = 8704
N_SEG = 8
N_TENSOR = 4


def draw_tokens(key, part):
    key = jax.random.fold_in(key, 1)
    initial_key = jax.random.fold_in(key, 0)
    value_rows = jnp.clip(jax.random.normal(initial_key, (TOKENS, MODEL_WIDTH)), -6.0, 6.0)
    return value_rows.astype(jnp.bfloat16)


def draw_w_query(key, part):
    key = jax.random.fold_in(key, 2)
    initial_key = jax.random.fold_in(key, 0)
    spread_deviation = MODEL_WIDTH ** (-0.5)
    value_rows = jnp.clip(jax.random.normal(initial_key, (MODEL_WIDTH, HQ * HEAD_SIZE)), -6.0, 6.0) * spread_deviation
    return value_rows.astype(jnp.bfloat16)


def draw_w_key(key, part):
    key = jax.random.fold_in(key, 3)
    initial_key = jax.random.fold_in(key, 0)
    spread_deviation = MODEL_WIDTH ** (-0.5)
    value_rows = jnp.clip(jax.random.normal(initial_key, (MODEL_WIDTH, KEY_VALUE_HEADS * HEAD_SIZE)), -6.0, 6.0) * spread_deviation
    return value_rows.astype(jnp.bfloat16)


def levels(stream_key, extent, pieces, low, high):
    level = 1.0
    for position, blocks in pieces:
        heights = jax.random.uniform(jax.random.fold_in(jax.random.fold_in(stream_key, 6), position), (blocks,), jnp.float32, low / len(pieces), high / len(pieces))
        level = level * jnp.repeat(jnp.exp(heights), extent[position] // blocks).reshape((-1,) + (1,) * (len(extent) - 1 - position))
    return level


def gaussian(key, extent, width, most, cuts=(), kind=jnp.bfloat16):
    array = jax.random.normal(key, extent, jnp.float32) * width
    if len(cuts) > 0:
        array = levels(key, extent, cuts, -0.22, 0.18) * array
    return jnp.clip(array, min=-most, max=most).astype(kind)


def setup_inputs(seed: int = 0) -> dict:
    key_list = jax.random.split(jax.random.key(seed), 9)
    tokens = draw_tokens(jax.random.fold_in(key_list[8], 71), 0)
    memory_embed = gaussian(key_list[1], (MEM, MODEL_WIDTH), 1.0, 6.0, ((0, 4),))
    norm_gain = jnp.clip(1.0 + 0.1 * jax.random.normal(key_list[2], (MODEL_WIDTH,), jnp.float32), 0.5, 1.5).astype(jnp.bfloat16)
    w_query = draw_w_query(jax.random.fold_in(key_list[8], 71), 0)
    w_key = draw_w_key(jax.random.fold_in(key_list[8], 71), 0)
    value_weight = gaussian(key_list[5], (MODEL_WIDTH, KEY_VALUE_HEADS * HEAD_SIZE), MODEL_WIDTH ** -0.5, 0.0625, ((1, 4),))
    w_out = gaussian(key_list[6], (HQ * HEAD_SIZE, MODEL_WIDTH), (HQ * HEAD_SIZE) ** -0.5, 0.09375, ((0, 4),))
    retain = jnp.clip(jnp.exp(math.log(1.0) - 2.9957323 * jax.random.uniform(key_list[7], (N_SEG, HQ), jnp.float32) ** levels(key_list[7], (N_SEG, HQ), ((0, 8), (1, 4)), -0.2, 0.2)), 0.05, 1.0)
    return {"tokens": tokens, "memory_embed": memory_embed, "norm_gain": norm_gain, "w_query": w_query, "w_key": w_key, "value_weight": value_weight, "w_out": w_out, "retain": retain}


epsilon = 1e-05

def rms_rows(rows, norm_gain):
    widened = rows.astype(jnp.float32)
    scale_rows = lax.rsqrt(lax.optimization_barrier(jnp.mean(widened * widened, axis=-1, keepdims=True)) + epsilon)
    return (widened * scale_rows * norm_gain.astype(jnp.float32)).astype(jnp.bfloat16)

def feature_map(inputs):
    return jax.nn.elu(inputs) + 1.0

def soft_part(queries, keys_all, values_all):
    count_rows = queries.shape[0]
    kv_heads = keys_all.shape[1] // HEAD_SIZE
    heads_query = queries.reshape(count_rows, kv_heads, -1, HEAD_SIZE).astype(jnp.float32)
    heads_key = keys_all.reshape(count_rows, kv_heads, HEAD_SIZE).astype(jnp.float32)
    heads_value = values_all.reshape(count_rows, kv_heads, HEAD_SIZE).astype(jnp.float32)
    scores = jnp.einsum('rkgd,ckd->kgrc', heads_query, heads_key) * HEAD_SIZE ** (-0.5)
    row_ids = lax.broadcasted_iota(jnp.int32, (count_rows, count_rows), 0)
    col_ids = lax.broadcasted_iota(jnp.int32, (count_rows, count_rows), 1)
    scores = jnp.where(row_ids >= col_ids, scores, -1e+30)
    top_score = lax.optimization_barrier(jnp.max(scores, axis=-1, keepdims=True))
    weights = jnp.exp(scores - top_score)
    probs = (weights / lax.optimization_barrier(jnp.sum(weights, axis=-1, keepdims=True))).astype(jnp.bfloat16)
    soft = jnp.einsum('kgrc,ckd->rkgd', probs.astype(jnp.float32), heads_value)
    return (soft, feature_map(heads_query), feature_map(heads_key))

def write_terms(soft, feat_key, tok_rows):
    mem_soft = soft[tok_rows:]
    mem_key = feat_key[tok_rows:]
    kv_heads = mem_soft.shape[1]
    groups = mem_soft.shape[2]
    write_mat = jnp.einsum('mkd,mkge->kgde', mem_key, mem_soft, precision=lax.Precision.HIGHEST)
    write_sum = jnp.broadcast_to(lax.optimization_barrier(jnp.sum(mem_key, axis=0))[:, None, :], (kv_heads, groups, HEAD_SIZE))
    return (write_mat.reshape(kv_heads * groups, HEAD_SIZE, HEAD_SIZE), write_sum.reshape(kv_heads * groups, HEAD_SIZE))

def read_terms(soft, feat_query, state_mat, state_sum, tok_rows):
    kv_heads = soft.shape[1]
    groups = soft.shape[2]
    state_four = state_mat.reshape(kv_heads, groups, HEAD_SIZE, HEAD_SIZE)
    sum_four = state_sum.reshape(kv_heads, groups, HEAD_SIZE)
    token_query = feat_query[:tok_rows]
    numerator = jnp.einsum('tkgd,kgde->tkge', token_query, state_four, precision=lax.Precision.HIGHEST)
    denominator = jnp.einsum('tkgd,kgd->tkg', token_query, sum_four, precision=lax.Precision.HIGHEST) + 1.0
    mixed = soft[:tok_rows] + numerator / denominator[..., None]
    return mixed.reshape(tok_rows, -1).astype(jnp.bfloat16)

def head_sum(mixed, w_out):
    group_cols = HQ // N_TENSOR * HEAD_SIZE
    summed_rows = jnp.zeros((mixed.shape[0], w_out.shape[1]), jnp.float32)
    for group_index in range(N_TENSOR):
        lower = group_index * group_cols
        group_part = jnp.dot(mixed[:, lower:lower + group_cols], w_out[lower:lower + group_cols], preferred_element_type=jnp.float32).astype(jnp.bfloat16)
        summed_rows = summed_rows + lax.optimization_barrier(group_part).astype(jnp.float32)
    return summed_rows

def reference(tokens, memory_embed, norm_gain, w_query, w_key, value_weight, w_out, retain):
    segments = tokens.reshape(N_SEG, SEG, MODEL_WIDTH)

    def segment_step(state_pair, inputs):
        state_mat, state_sum = state_pair
        seg_tokens, keep_rates = inputs
        normed = rms_rows(jnp.concatenate([seg_tokens, memory_embed], axis=0), norm_gain)
        queries = jnp.dot(normed, w_query, preferred_element_type=jnp.float32).astype(jnp.bfloat16)
        keys_all = jnp.dot(normed, w_key, preferred_element_type=jnp.float32).astype(jnp.bfloat16)
        values_all = jnp.dot(normed, value_weight, preferred_element_type=jnp.float32).astype(jnp.bfloat16)
        soft, feat_query, feat_key = soft_part(queries, keys_all, values_all)
        write_mat, write_sum = write_terms(soft, feat_key, SEG)
        mixed = read_terms(soft, feat_query, state_mat, state_sum, SEG)
        summed = head_sum(mixed, w_out)
        result = (seg_tokens.astype(jnp.float32) + summed).astype(jnp.bfloat16)
        next_mat = keep_rates[:, None, None] * state_mat + write_mat
        next_sum = keep_rates[:, None] * state_sum + write_sum
        return ((next_mat, next_sum), result)
    start_state = (jnp.zeros((HQ, HEAD_SIZE, HEAD_SIZE), jnp.float32), jnp.zeros((HQ, HEAD_SIZE), jnp.float32))
    _, outputs = lax.scan(segment_step, start_state, (segments, retain))
    return outputs.reshape(N_SEG * SEG, MODEL_WIDTH)
```

```python
import functools

import jax
import jax.numpy as jnp
from jax import lax
from jax.experimental import pallas as pl
from jax.experimental.pallas import tpu as pltpu
from jax.sharding import PartitionSpec as P

HEAD = 128
EPSILON = 1e-05
SCALE = HEAD ** (-0.5)
LOG2E = 1.4426950408889634
STATE_ROWS = HEAD + 16
VMEM_LIMIT = 48 * 1024 * 1024


def rms_rows(rows, norm_gain):
    widened = rows.astype(jnp.float32)
    scale_rows = lax.rsqrt(jnp.mean(widened * widened, axis=-1, keepdims=True) + EPSILON)
    return (widened * scale_rows * norm_gain.astype(jnp.float32)).astype(jnp.bfloat16)


def feature_map(inputs):
    return jnp.exp(jnp.minimum(inputs, 0.0)) + jnp.maximum(inputs, 0.0)


def after(value, *others):
    return lax.optimization_barrier((value,) + others)[0]


class Planes:
    def __init__(self, count):
        self.count = count
        self.quarter = count // 4
        self.workers = range(self.quarter, 3 * self.quarter)
        self.ends = [i for i in range(count) if i not in self.workers]
        self.turns = range(1, count // 2)

    def partner(self, index):
        return index ^ self.quarter

    def peer(self, index, turn):
        return self.quarter + ((index - self.quarter) ^ turn)

    def lend(self):
        return [(e, self.partner(e)) for e in self.ends]

    def give_back(self):
        return [(w, self.partner(w)) for w in self.workers]

    def pairs(self):
        return [(i, self.partner(i)) for i in range(self.count)]

    def exchange(self, turn):
        return [(w, self.peer(w, turn)) for w in self.workers]

    def far_back(self, turn):
        return [(w, self.partner(self.peer(w, turn))) for w in self.workers]


def hop(block, pairs):
    return lax.ppermute(block, "tensor", pairs)


def seg_cycle(chips):
    half = chips // 2
    return list(range(half)) + list(range(chips - 1, half - 1, -1))


def seg_gather(block):
    size = lax.axis_size("seg")
    chips = size // 2
    cycle = seg_cycle(chips)
    place_of = [cycle.index(c) for c in range(chips)]

    def step(part, distance):
        route = [
            (cycle[i] * 2 + c, cycle[(i + distance) % chips] * 2 + c)
            for i in range(chips)
            for c in range(2)
        ]
        return lax.ppermute(part, "seg", route)

    me = lax.axis_index("seg")
    chip, core = me // 2, me % 2
    place = jnp.array(place_of, jnp.int32)[chip]
    cycle_table = jnp.array(cycle, jnp.int32)

    found = [((block,), 0)]
    right = left = block
    for turn in range(1, chips // 2):
        right, left = step(right, 1), step(left, -1)
        found += [((right,), -turn), ((left,), turn)]
    half = block.shape[0] // 2
    found.append(((step(right[:half], 1), step(left[half:], -1)), chips // 2))
    swap = [(i, i ^ 1) for i in range(size)]
    result = []
    for parts, distance in found:
        owner = cycle_table[(place + distance + chips) % chips] * 2
        result.append((parts, owner + core))
        other = tuple(lax.ppermute(p, "seg", swap) for p in parts)
        result.append((other, owner + 1 - core))
    return result


def seg_slice(array, axis):
    width = array.shape[axis] // lax.axis_size("seg")
    return lax.dynamic_slice_in_dim(array, lax.axis_index("seg") * width, width, axis)


def pad_to(value, unit):
    return -(-value // unit) * unit


def fill(place_ref, slot_refs, all_ref, stride, rows):
    for i, ref in enumerate(slot_refs):
        start = pl.multiple_of(place_ref[i] * stride, 16)
        all_ref[pl.ds(start, rows), :] = ref[...]


def nt_dot(a, b):
    return lax.dot_general(a, b, (((1,), (1,)), ((), ())), preferred_element_type=jnp.float32)


def memory_kernel(slots, stride, rows, groups, place_ref, *refs):
    keys, values = refs[:slots], refs[slots : 2 * slots]
    mem_q, mem_k, mem_v, out_ref, key_all, value_all = refs[2 * slots :]
    mem = mem_k.shape[0]
    base = slots * stride
    if stride != rows:
        key_all[...] = jnp.zeros_like(key_all)
        value_all[...] = jnp.zeros_like(value_all)
    fill(place_ref, keys, key_all, stride, rows)
    fill(place_ref, values, value_all, stride, rows)
    k_tok, v_tok = key_all[...], value_all[...]
    k_mem, v_mem = mem_k[...], mem_v[...]
    row_ids = lax.broadcasted_iota(jnp.int32, (mem, mem), 0)
    col_ids = lax.broadcasted_iota(jnp.int32, (mem, mem), 1)
    feat = feature_map(k_mem.astype(jnp.float32))
    feat_sum = jnp.sum(feat, axis=0, keepdims=True)
    feat_cast = feat.astype(jnp.bfloat16)
    for g in range(groups):
        q = mem_q[:, g * HEAD : (g + 1) * HEAD]
        s_tok = nt_dot(q, k_tok)
        if stride != rows:
            ids = lax.broadcasted_iota(jnp.int32, (mem, base), 1)
            s_tok = jnp.where(lax.rem(ids, stride) < rows, s_tok, -1e30)
        s_mem = jnp.where(row_ids >= col_ids, nt_dot(q, k_mem), -1e30)
        top = jnp.maximum(
            jnp.max(s_tok, axis=1, keepdims=True), jnp.max(s_mem, axis=1, keepdims=True)
        )
        p_tok = jnp.exp2((s_tok - top) * (SCALE * LOG2E))
        p_mem = jnp.exp2((s_mem - top) * (SCALE * LOG2E))
        total = jnp.sum(p_tok, axis=1, keepdims=True) + jnp.sum(p_mem, axis=1, keepdims=True)
        soft = jnp.dot(
            p_tok.astype(jnp.bfloat16), v_tok, preferred_element_type=jnp.float32
        ) + jnp.dot(p_mem.astype(jnp.bfloat16), v_mem, preferred_element_type=jnp.float32)
        soft = soft / total
        out_ref[g, :HEAD, :] = lax.dot_general(
            feat_cast,
            soft.astype(jnp.bfloat16),
            (((0,), (0,)), ((), ())),
            preferred_element_type=jnp.float32,
        )
        out_ref[g, HEAD:, :] = jnp.broadcast_to(feat_sum, (STATE_ROWS - HEAD, HEAD))


def token_kernel(slots, stride, rows, groups, place_ref, *refs):
    queries, keys, values = refs[:slots], refs[slots : 2 * slots], refs[2 * slots : 3 * slots]
    outs = refs[3 * slots : 4 * slots]
    query_all, key_all, value_all, out_all = refs[4 * slots :]
    full = key_all.shape[0]
    if stride != rows:
        query_all[...] = jnp.zeros_like(query_all)
        key_all[...] = jnp.zeros_like(key_all)
        value_all[...] = jnp.zeros_like(value_all)
    elif full > slots * stride:
        tail = (full - slots * stride, HEAD)
        key_all[slots * stride :, :] = jnp.zeros(tail, key_all.dtype)
        value_all[slots * stride :, :] = jnp.zeros(tail, value_all.dtype)
    fill(place_ref, queries, query_all, stride, rows)
    fill(place_ref, keys, key_all, stride, rows)
    fill(place_ref, values, value_all, stride, rows)

    for block in range(slots):
        first = block * stride
        low = first // 128 * 128
        high = min(pad_to(first + stride, 128), full)
        k_diag, v_diag = key_all[low:high, :], value_all[low:high, :]
        row_ids = lax.broadcasted_iota(jnp.int32, (stride, high - low), 0) + first
        col_ids = lax.broadcasted_iota(jnp.int32, (stride, high - low), 1) + low
        keep = row_ids >= col_ids
        if stride != rows:
            keep = keep & (lax.rem(col_ids, stride) < rows)

        def one_head(g, carry, first=first, low=low, k_diag=k_diag, v_diag=v_diag, keep=keep):
            lanes = pl.ds(pl.multiple_of(g * HEAD, HEAD), HEAD)
            q = query_all[first : first + stride, lanes]
            s_diag = jnp.where(keep, nt_dot(q, k_diag), -1e30)
            top = jnp.max(s_diag, axis=1, keepdims=True)
            if low > 0:
                s_prev = nt_dot(q, key_all[:low, :])
                if stride != rows:
                    ids = lax.broadcasted_iota(jnp.int32, (stride, low), 1)
                    s_prev = jnp.where(lax.rem(ids, stride) < rows, s_prev, -1e30)
                top = jnp.maximum(top, jnp.max(s_prev, axis=1, keepdims=True))
            p_diag = jnp.exp2((s_diag - top) * (SCALE * LOG2E))
            total = jnp.sum(p_diag, axis=1, keepdims=True)
            soft = jnp.dot(
                p_diag.astype(jnp.bfloat16), v_diag, preferred_element_type=jnp.float32
            )
            if low > 0:
                p_prev = jnp.exp2((s_prev - top) * (SCALE * LOG2E))
                total = total + jnp.sum(p_prev, axis=1, keepdims=True)
                soft = soft + jnp.dot(
                    p_prev.astype(jnp.bfloat16),
                    value_all[:low, :],
                    preferred_element_type=jnp.float32,
                )
            out_all[first : first + stride, lanes] = soft / total
            return carry

        lax.fori_loop(0, groups, one_head, 0)

    for i, ref in enumerate(outs):
        start = pl.multiple_of(place_ref[i] * stride, 16)
        ref[...] = out_all[pl.ds(start, rows), :]


def read_kernel(slots, *refs):
    softs, queries = refs[:slots], refs[slots : 2 * slots]
    state_ref = refs[2 * slots]
    outs = refs[2 * slots + 1 :]
    state = state_ref[0, :HEAD, :].astype(jnp.bfloat16)
    sums = jnp.broadcast_to(state_ref[0, HEAD : HEAD + 1, :], (HEAD, HEAD)).astype(jnp.bfloat16)
    for soft, query, out in zip(softs, queries, outs):
        feat = feature_map(query[...].astype(jnp.float32)).astype(jnp.bfloat16)
        numerator = jnp.dot(feat, state, preferred_element_type=jnp.float32)
        denominator = nt_dot(feat, sums) + 1.0
        out[...] = (soft[...] + numerator / denominator).astype(jnp.bfloat16)


class Group:
    def __init__(self, queries, keys, values, key_block, value_block, mem, heads, kv_heads):
        self.queries, self.keys, self.values = queries, keys, values
        self.key_block, self.value_block = key_block, value_block
        self.mem = mem
        self.heads, self.kv_heads = heads, kv_heads
        self.groups = heads // kv_heads
        self.rows = queries[0].shape[0]
        self.stride = pad_to(self.rows, 16)

    def specs(self, rows):
        wide = self.groups * HEAD
        kb, vb = self.key_block, self.value_block
        return (
            pl.BlockSpec((rows, wide), lambda h, *_: (0, h)),
            pl.BlockSpec((rows, HEAD), lambda h, *_: (0, h + kb)),
            pl.BlockSpec((rows, HEAD), lambda h, *_: (0, h + vb)),
        )

    def write(self, places):
        slots = len(self.keys)
        _, k_spec, v_spec = self.specs(self.rows)
        mem_rows = self.mem[0].shape[0]
        spread = slots * self.stride
        return pl.pallas_call(
            functools.partial(memory_kernel, slots, self.stride, self.rows, self.groups),
            grid_spec=pltpu.PrefetchScalarGridSpec(
                num_scalar_prefetch=1,
                grid=(self.kv_heads,),
                in_specs=[k_spec] * slots + [v_spec] * slots + list(self.specs(mem_rows)),
                out_specs=pl.BlockSpec((self.groups, STATE_ROWS, HEAD), lambda h, *_: (h, 0, 0)),
                scratch_shapes=[
                    pltpu.VMEM((spread, HEAD), jnp.bfloat16),
                    pltpu.VMEM((spread, HEAD), jnp.bfloat16),
                ],
            ),
            out_shape=jax.ShapeDtypeStruct((self.heads, STATE_ROWS, HEAD), jnp.float32),
            compiler_params=pltpu.CompilerParams(vmem_limit_bytes=VMEM_LIMIT),
            name="memory_write",
        )(places, *self.keys, *self.values, *self.mem)

    def attend(self, places):
        slots = len(self.keys)
        wide = self.groups * HEAD
        q_spec, k_spec, v_spec = self.specs(self.rows)
        spread = slots * self.stride
        full = pad_to(spread, 128)
        work = 2 * self.heads * spread * spread * HEAD
        return pl.pallas_call(
            functools.partial(token_kernel, slots, self.stride, self.rows, self.groups),
            grid_spec=pltpu.PrefetchScalarGridSpec(
                num_scalar_prefetch=1,
                grid=(self.kv_heads,),
                in_specs=[q_spec] * slots + [k_spec] * slots + [v_spec] * slots,
                out_specs=[pl.BlockSpec((self.rows, wide), lambda h, *_: (0, h))] * slots,
                scratch_shapes=[
                    pltpu.VMEM((spread, wide), jnp.bfloat16),
                    pltpu.VMEM((full, HEAD), jnp.bfloat16),
                    pltpu.VMEM((full, HEAD), jnp.bfloat16),
                    pltpu.VMEM((spread, wide), jnp.float32),
                ],
            ),
            out_shape=[jax.ShapeDtypeStruct((self.rows, self.heads * HEAD), jnp.float32)] * slots,
            compiler_params=pltpu.CompilerParams(vmem_limit_bytes=VMEM_LIMIT),
            cost_estimate=pl.CostEstimate(
                flops=2 * work, bytes_accessed=16 * spread * wide, transcendentals=work // 256
            ),
            name="token_attention",
        )(places, *self.queries, *self.keys, *self.values)

    def read(self, softs, state):
        slots = len(softs)
        block = pl.BlockSpec((self.rows, HEAD), lambda h: (0, h))
        return pl.pallas_call(
            functools.partial(read_kernel, slots),
            grid=(self.heads,),
            in_specs=[block] * (2 * slots)
            + [pl.BlockSpec((1, STATE_ROWS, HEAD), lambda h: (h, 0, 0))],
            out_specs=[block] * slots,
            out_shape=[jax.ShapeDtypeStruct((self.rows, self.heads * HEAD), jnp.bfloat16)] * slots,
            compiler_params=pltpu.CompilerParams(vmem_limit_bytes=VMEM_LIMIT),
            name="memory_read",
        )(*softs, *self.queries, state)


def relay(writes, rates):
    size = lax.axis_size("seg")
    me = lax.axis_index("seg")
    ids = lax.broadcasted_iota(jnp.int32, (size, 1), 0)

    def product(mask):
        return jnp.prod(jnp.where(mask, rates, 1.0), axis=0)[:, None, None]

    total = writes
    prefix = jnp.zeros_like(writes)
    bit = 1
    while bit < size:
        route = [(i, i ^ bit) for i in range(size)]
        got = lax.ppermute(total.astype(jnp.bfloat16), "seg", route).astype(jnp.float32)
        mine = ids // bit == me // bit
        theirs = ids // bit == (me // bit) ^ 1
        upper = (me // bit) % 2 == 1
        prefix = jnp.where(upper, product(mine & (ids < me)) * got + prefix, prefix)
        total = jnp.where(upper, product(mine) * got + total, product(theirs) * total + got)
        bit *= 2
    return prefix


def output_kernel(plan, bufs, ids_ref, mixed_ref, tokens_ref, own_ref, *refs):
    count = sum(len(p) for row in plan for p in row if p is not None)
    piece_refs, (out_ref, weights, total, sems) = refs[:count], refs[count:]
    blocks, groups = len(plan), len(plan[0])
    width = weights.shape[2]
    c, g = pl.program_id(0), pl.program_id(1)
    step = c * groups + g
    steps = blocks * groups

    def start(at):
        slot = lax.rem(at, bufs)
        for b in range(blocks):
            for j in range(groups):

                @pl.when(at == b * groups + j)
                def _():
                    if plan[b][j] is None:
                        columns = pl.ds(pl.multiple_of(ids_ref[b] * width, 128), width)
                        pltpu.make_async_copy(
                            own_ref.at[:, columns], weights.at[slot], sems.at[slot]
                        ).start()
                        return
                    row = 0
                    for index in plan[b][j]:
                        part = piece_refs[index]
                        high = part.shape[0]
                        pltpu.make_async_copy(
                            part, weights.at[slot, pl.ds(row, high), :], sems.at[slot]
                        ).start()
                        row += high

    @pl.when(step == 0)
    def _():
        for at in range(min(bufs - 1, steps)):
            start(jnp.int32(at))

    @pl.when(step + bufs - 1 < steps)
    def _():
        start(step + bufs - 1)

    slot = lax.rem(step, bufs)
    pltpu.make_async_copy(weights.at[slot], weights.at[slot], sems.at[slot]).wait()
    term = jnp.dot(mixed_ref[g], weights[slot], preferred_element_type=jnp.float32)

    @pl.when(g == 0)
    def _():
        total[...] = tokens_ref[...].astype(jnp.float32) + term

    @pl.when(g > 0)
    def _():
        total[...] = total[...] + term

    @pl.when(g == groups - 1)
    def _():
        out_ref[...] = total[...].astype(out_ref.dtype)


def output_product(mixed, tokens, w_out, gathered):
    groups, rows, depth = mixed.shape
    blocks = len(gathered[0])
    width = w_out.shape[1] // blocks
    ids = jnp.stack([gathered[0][b][1] for b in range(blocks)]).astype(jnp.int32)
    plan, pieces = [], []
    for b in range(blocks):
        row = [None]
        for pieces_of in gathered:
            parts = pieces_of[b][0]
            row.append(tuple(range(len(pieces), len(pieces) + len(parts))))
            pieces += parts
        plan.append(row)
    bufs = 4
    return pl.pallas_call(
        functools.partial(output_kernel, plan, bufs),
        grid_spec=pltpu.PrefetchScalarGridSpec(
            num_scalar_prefetch=1,
            grid=(blocks, groups),
            in_specs=[
                pl.BlockSpec((groups, rows, depth), lambda c, g, ids: (0, 0, 0)),
                pl.BlockSpec((rows, width), lambda c, g, ids: (0, ids[c])),
                pl.BlockSpec(memory_space=pl.ANY),
            ]
            + [pl.BlockSpec(memory_space=pl.ANY)] * len(pieces),
            out_specs=pl.BlockSpec((rows, width), lambda c, g, ids: (0, ids[c])),
            scratch_shapes=[
                pltpu.VMEM((bufs, depth, width), jnp.bfloat16),
                pltpu.VMEM((rows, width), jnp.float32),
                pltpu.SemaphoreType.DMA((bufs,)),
            ],
        ),
        out_shape=jax.ShapeDtypeStruct(tokens.shape, tokens.dtype),
        compiler_params=pltpu.CompilerParams(vmem_limit_bytes=VMEM_LIMIT),
        name="output_product",
    )(ids, mixed, tokens, w_out, *pieces)


def dot_cast(a, b):
    return jnp.dot(a, b, preferred_element_type=jnp.float32).astype(jnp.bfloat16)


def per_device(tokens, memory_embed, norm_gain, w_query, w_key, value_weight, w_out, retain):
    planes = Planes(lax.axis_size("tensor"))
    me = lax.axis_index("tensor")
    is_worker = (me >= planes.quarter) & (me < 3 * planes.quarter)
    is_end = jnp.logical_not(is_worker)
    worker = jnp.where(is_end, planes.partner(me), me)
    rows = tokens.shape[0]
    width = tokens.shape[1]
    seg_count = lax.axis_size("seg")
    heads, kv_heads = w_query.shape[1] // HEAD, w_key.shape[1] // HEAD

    normed = rms_rows(tokens, norm_gain)
    mem_local = rms_rows(memory_embed, norm_gain)

    lent = jnp.concatenate(
        [seg_slice(w_query, 0), seg_slice(w_key, 0), seg_slice(value_weight, 0)], axis=1
    )
    lent = hop(lent, planes.lend())
    lent_pieces = seg_gather(lent)

    slots = [normed]
    places = [me, planes.partner(me)]
    slots.append(hop(normed, planes.lend()))
    for turn in planes.turns:
        peer = planes.peer(worker, turn)
        slots.append(hop(normed, planes.exchange(turn)))
        slots.append(hop(slots[1], planes.exchange(turn)))
        places += [peer, planes.partner(peer)]
    places = jnp.stack(places).astype(jnp.int32)

    mem_slice = seg_slice(mem_local, 1)
    mem_all = lax.all_gather(mem_slice, "tensor", axis=0, tiled=True)
    mem_all = lax.all_gather(mem_all, "seg", axis=1, tiled=True)
    mem_rows = mem_all.shape[0]

    share = seg_slice(w_out, 1)
    near = hop(share, planes.pairs())
    shares = [near]
    for turn in planes.turns:
        for piece in (share, near):
            piece = hop(piece, planes.exchange(turn))
            shares.append(jnp.where(is_end, hop(piece, planes.give_back()), piece))
    gathered = [seg_gather(piece) for piece in shares]

    rates = lax.all_gather(retain[0], "seg", axis=0)
    rates = jnp.concatenate([rates, hop(rates, planes.lend())], axis=1)

    lent_all = jnp.zeros((width, lent.shape[1]), jnp.bfloat16)
    piece_rows = width // seg_count
    for parts, owner in lent_pieces:
        start = owner * piece_rows
        for part in parts:
            lent_all = lax.dynamic_update_slice(lent_all, part, (start, 0))
            start = start + part.shape[0]

    first = jnp.concatenate([normed, mem_all], axis=0)
    inputs = [first] + slots[1:]
    own_q = [dot_cast(x, w_query) for x in inputs]
    own_k = [dot_cast(x, w_key) for x in inputs]
    own_v = [dot_cast(x, value_weight) for x in inputs]
    lent_qkv = [dot_cast(x, lent_all) for x in inputs]

    def split(arrays):
        return [arrays[0][:rows]] + arrays[1:], arrays[0][rows:]

    (own_q, mem_q), (own_k, mem_k), (own_v, mem_v) = split(own_q), split(own_k), split(own_v)
    lent_qkv, mem_qkv = split(lent_qkv)
    own = Group(own_q, own_k, own_v, 0, 0, (mem_q, mem_k, mem_v), heads, kv_heads)
    lent = Group(
        lent_qkv,
        lent_qkv,
        lent_qkv,
        heads,
        heads + kv_heads,
        (mem_qkv, mem_qkv, mem_qkv),
        heads,
        kv_heads,
    )

    writes = jnp.concatenate([own.write(places), lent.write(places)], axis=0)
    state = relay(writes, rates)
    mixed_own = own.read(own.attend(places), state[:heads])
    mixed_lent = lent.read(lent.attend(places), state[heads:])

    back = planes.give_back()
    mixed = [
        jnp.where(is_end, hop(mixed_lent[1], back), mixed_own[0]),
        jnp.where(is_end, hop(mixed_own[1], back), mixed_lent[0]),
    ]
    for number, turn in enumerate(planes.turns):
        near_slot, far_slot = 2 + 2 * number, 3 + 2 * number
        for arrays in (mixed_own, mixed_lent):
            mixed.append(
                jnp.where(
                    is_end,
                    hop(arrays[far_slot], planes.far_back(turn)),
                    hop(arrays[near_slot], planes.exchange(turn)),
                )
            )
    return output_product(jnp.stack(mixed), tokens, w_out, gathered)


def solution(mesh):
    return jax.shard_map(
        per_device,
        mesh=mesh,
        in_specs=(
            P(("seg", "tensor"), None),
            P("tensor", None),
            P(),
            P(None, "tensor"),
            P(None, "tensor"),
            P(None, "tensor"),
            P("tensor", None),
            P("seg", "tensor"),
        ),
        out_specs=P(("seg", "tensor"), None),
        check_vma=False,
    )
```

```python
import functools

import jax
import jax.numpy as jnp
from jax import lax
from jax.experimental import pallas as pl
from jax.experimental.pallas import tpu as pltpu
from jax.sharding import PartitionSpec as P

HEAD = 128
EPSILON = 1e-05
SCALE = HEAD ** (-0.5)
LOG2E = 1.4426950408889634
STATE_ROWS = HEAD + 16
VMEM_LIMIT = 48 * 1024 * 1024
SMALL = pl.CostEstimate(flops=1, bytes_accessed=1, transcendentals=0)


def rms_rows(rows, norm_gain):
    widened = rows.astype(jnp.float32)
    scale_rows = lax.rsqrt(jnp.mean(widened * widened, axis=-1, keepdims=True) + EPSILON)
    return (widened * scale_rows * norm_gain.astype(jnp.float32)).astype(jnp.bfloat16)


def feature_map(inputs):
    return jnp.exp(jnp.minimum(inputs, 0.0)) + jnp.maximum(inputs, 0.0)


def tie(value, *others):
    return lax.optimization_barrier((value,) + others)[0]


def gate(*values):
    return lax.optimization_barrier(values)


class Planes:
    def __init__(self, count):
        self.count = count
        self.quarter = count // 4
        self.workers = range(self.quarter, 3 * self.quarter)
        self.ends = [i for i in range(count) if i not in self.workers]
        self.turns = range(1, count // 2)

    def partner(self, index):
        return index ^ self.quarter

    def peer(self, index, turn):
        return self.quarter + ((index - self.quarter) ^ turn)

    def lend(self):
        return [(e, self.partner(e)) for e in self.ends]

    def give_back(self):
        return [(w, self.partner(w)) for w in self.workers]

    def pairs(self):
        return [(i, self.partner(i)) for i in range(self.count)]

    def exchange(self, turn):
        return [(w, self.peer(w, turn)) for w in self.workers]

    def far_back(self, turn):
        return [(w, self.partner(self.peer(w, turn))) for w in self.workers]


def hop(block, pairs):
    return lax.ppermute(block, "tensor", pairs)


def seg_cycle(chips):
    half = chips // 2
    return list(range(half)) + list(range(chips - 1, half - 1, -1))


def swap_cores(block):
    return lax.ppermute(block, "seg", [(i, i ^ 1) for i in range(lax.axis_size("seg"))])


class ChipRing:
    def __init__(self, block):
        self.chips = lax.axis_size("seg") // 2
        self.cycle = seg_cycle(self.chips)
        self.block, self.right, self.left = block, [block], [block]
        for _ in range(1, self.chips // 2):
            self.right.append(self.step(self.right[-1], 1))
            self.left.append(self.step(self.left[-1], -1))

    def step(self, part, distance):
        route = [
            (self.cycle[i] * 2 + c, self.cycle[(i + distance) % self.chips] * 2 + c)
            for i in range(self.chips)
            for c in range(2)
        ]
        return lax.ppermute(part, "seg", route)

    def close(self):
        half = self.block.shape[0] // 2
        self.last = (self.step(self.right[-1][:half], 1), self.step(self.left[-1][half:], -1))
        return self.last

    def pieces(self):
        place_of = [self.cycle.index(c) for c in range(self.chips)]
        place = jnp.array(place_of, jnp.int32)[lax.axis_index("seg") // 2]
        table = jnp.array(self.cycle, jnp.int32)
        found = [((self.block,), 0)]
        for turn in range(1, self.chips // 2):
            found += [((self.right[turn],), -turn), ((self.left[turn],), turn)]
        found.append((self.last, self.chips // 2))
        return [(parts, table[(place + at + self.chips) % self.chips]) for parts, at in found]


def seg_all(values):
    size = lax.axis_size("seg")
    me = lax.axis_index("seg")
    bit = 1
    while bit < size:
        got = lax.ppermute(values, "seg", [(i, i ^ bit) for i in range(size)])
        upper = (me // bit) % 2 == 1
        values = jnp.concatenate(
            [jnp.where(upper, got, values), jnp.where(upper, values, got)], axis=0
        )
        bit *= 2
    return values


def pad_to(value, unit):
    return -(-value // unit) * unit


def pad_rows(array, unit=16):
    return jnp.pad(array, ((0, pad_to(array.shape[0], unit) - array.shape[0]), (0, 0)))


def nt_dot(a, b):
    return lax.dot_general(a, b, (((1,), (1,)), ((), ())), preferred_element_type=jnp.float32)


class Layout:
    def __init__(self, slots, rows, mem, groups):
        self.slots, self.rows, self.mem, self.groups = slots, rows, mem, groups
        self.stride, self.mem_stride = pad_to(rows, 16), pad_to(mem, 16)
        self.height = self.stride + self.mem_stride
        self.spread = slots * self.stride
        self.mem_spread = slots * self.mem_stride
        self.full = pad_to(self.spread, 128)
        self.wide = groups * HEAD
        self.unit = (groups + 2) * HEAD

    def valid(self, ids):
        return lax.rem(ids, self.stride) < self.rows

    def mem_valid(self, ids):
        return lax.rem(ids, self.mem_stride) < self.mem


def memory_kernel(lay, place_ref, *refs):
    slots, out_ref, key_all, value_all, mem_all = refs[: lay.slots], *refs[lay.slots :]
    wide = lay.wide
    for i, ref in enumerate(slots):
        start = pl.multiple_of(place_ref[i] * lay.stride, 16)
        key_all[pl.ds(start, lay.stride), :] = ref[: lay.stride, wide : wide + HEAD]
        value_all[pl.ds(start, lay.stride), :] = ref[: lay.stride, wide + HEAD :]
        start = pl.multiple_of(place_ref[i] * lay.mem_stride, 16)
        mem_all[pl.ds(start, lay.mem_stride), :] = ref[lay.stride :, :]
    k_tok, v_tok = key_all[...], value_all[...]
    k_mem, v_mem = mem_all[:, wide : wide + HEAD], mem_all[:, wide + HEAD :]
    mem = lay.mem_spread
    row_ids = lax.broadcasted_iota(jnp.int32, (mem, mem), 0)
    col_ids = lax.broadcasted_iota(jnp.int32, (mem, mem), 1)
    keep = row_ids >= col_ids
    feat = feature_map(k_mem.astype(jnp.float32))
    if lay.mem_stride != lay.mem:
        keep = keep & lay.mem_valid(col_ids)
        feat_ids = lax.broadcasted_iota(jnp.int32, (mem, HEAD), 0)
        feat = jnp.where(lay.mem_valid(feat_ids), feat, 0.0)
    feat_sum = jnp.sum(feat, axis=0, keepdims=True)
    feat_cast = feat.astype(jnp.bfloat16)
    for g in range(lay.groups):
        q = mem_all[:, g * HEAD : (g + 1) * HEAD]
        s_tok = nt_dot(q, k_tok)
        if lay.stride != lay.rows:
            ids = lax.broadcasted_iota(jnp.int32, (mem, lay.spread), 1)
            s_tok = jnp.where(lay.valid(ids), s_tok, -1e30)
        s_mem = jnp.where(keep, nt_dot(q, k_mem), -1e30)
        top = jnp.maximum(
            jnp.max(s_tok, axis=1, keepdims=True), jnp.max(s_mem, axis=1, keepdims=True)
        )
        p_tok = jnp.exp2((s_tok - top) * (SCALE * LOG2E))
        p_mem = jnp.exp2((s_mem - top) * (SCALE * LOG2E))
        total = jnp.sum(p_tok, axis=1, keepdims=True) + jnp.sum(p_mem, axis=1, keepdims=True)
        soft = jnp.dot(
            p_tok.astype(jnp.bfloat16), v_tok, preferred_element_type=jnp.float32
        ) + jnp.dot(p_mem.astype(jnp.bfloat16), v_mem, preferred_element_type=jnp.float32)
        soft = soft / total
        out_ref[g, :HEAD, :] = lax.dot_general(
            feat_cast,
            soft.astype(jnp.bfloat16),
            (((0,), (0,)), ((), ())),
            preferred_element_type=jnp.float32,
        )
        out_ref[g, HEAD:, :] = jnp.broadcast_to(feat_sum, (STATE_ROWS - HEAD, HEAD))


def read_state(query, state, sums):
    feat = feature_map(query.astype(jnp.float32)).astype(jnp.bfloat16)
    numerator = jnp.dot(feat, state.astype(jnp.bfloat16), preferred_element_type=jnp.float32)
    sums = jnp.broadcast_to(sums, (HEAD, HEAD)).astype(jnp.bfloat16)
    return numerator / (nt_dot(feat, sums) + 1.0)


def token_kernel(lay, begun, place_ref, *refs):
    count, stride, wide = lay.slots, lay.stride, lay.wide
    slots, refs = refs[:count], refs[count:]
    state_ref, refs = refs[0], refs[1 + begun :]
    outs, (query_all, key_all, value_all, out_all) = refs[:count], refs[count:]
    if lay.full > lay.spread:
        tail = (lay.full - lay.spread, HEAD)
        key_all[lay.spread :, :] = jnp.zeros(tail, key_all.dtype)
        value_all[lay.spread :, :] = jnp.zeros(tail, value_all.dtype)
    for i, ref in enumerate(slots):
        rows = pl.ds(pl.multiple_of(place_ref[i] * stride, 16), stride)
        query_all[rows, :] = ref[:stride, :wide]
        key_all[rows, :] = ref[:stride, wide : wide + HEAD]
        value_all[rows, :] = ref[:stride, wide + HEAD :]

    for block in range(count):
        first = block * stride
        low = first // 128 * 128
        high = min(pad_to(first + stride, 128), lay.full)
        k_diag, v_diag = key_all[low:high, :], value_all[low:high, :]
        row_ids = lax.broadcasted_iota(jnp.int32, (stride, high - low), 0) + first
        col_ids = lax.broadcasted_iota(jnp.int32, (stride, high - low), 1) + low
        keep = row_ids >= col_ids
        if stride != lay.rows:
            keep = keep & lay.valid(col_ids)

        def one_head(g, carry, first=first, low=low, k_diag=k_diag, v_diag=v_diag, keep=keep):
            lanes = pl.ds(pl.multiple_of(g * HEAD, HEAD), HEAD)
            q = query_all[first : first + stride, lanes]
            s_diag = jnp.where(keep, nt_dot(q, k_diag), -1e30)
            top = jnp.max(s_diag, axis=1, keepdims=True)
            if low > 0:
                s_prev = nt_dot(q, key_all[:low, :])
                if stride != lay.rows:
                    ids = lax.broadcasted_iota(jnp.int32, (stride, low), 1)
                    s_prev = jnp.where(lay.valid(ids), s_prev, -1e30)
                top = jnp.maximum(top, jnp.max(s_prev, axis=1, keepdims=True))
            p_diag = jnp.exp2((s_diag - top) * (SCALE * LOG2E))
            total = jnp.sum(p_diag, axis=1, keepdims=True)
            soft = jnp.dot(
                p_diag.astype(jnp.bfloat16), v_diag, preferred_element_type=jnp.float32
            )
            if low > 0:
                p_prev = jnp.exp2((s_prev - top) * (SCALE * LOG2E))
                total = total + jnp.sum(p_prev, axis=1, keepdims=True)
                soft = soft + jnp.dot(
                    p_prev.astype(jnp.bfloat16),
                    value_all[:low, :],
                    preferred_element_type=jnp.float32,
                )
            state, sums = state_ref[g, :HEAD, :], state_ref[g, HEAD : HEAD + 1, :]
            out_all[first : first + stride, lanes] = soft / total + read_state(q, state, sums)
            return carry

        lax.fori_loop(0, lay.groups, one_head, 0)

    for i, ref in enumerate(outs):
        rows = pl.ds(pl.multiple_of(place_ref[i] * stride, 16), stride)
        ref[...] = out_all[rows, :].astype(ref.dtype)


class Unit:
    def __init__(self, lay, places, slots, at=0):
        self.lay, self.places, self.slots, self.at = lay, places, slots, at

    def tied(self, *others):
        return Unit(self.lay, self.places, [tie(s, *others) for s in self.slots], self.at)

    def slot_specs(self):
        lay, at = self.lay, self.at
        return [pl.BlockSpec((lay.height, lay.unit), lambda i, *_: (0, at))] * lay.slots

    def state_spec(self):
        return pl.BlockSpec((self.lay.groups, STATE_ROWS, HEAD), lambda i, *_: (0, 0, 0))

    def memory_write(self):
        lay = self.lay
        return pl.pallas_call(
            functools.partial(memory_kernel, lay),
            grid_spec=pltpu.PrefetchScalarGridSpec(
                num_scalar_prefetch=1,
                grid=(1,),
                in_specs=self.slot_specs(),
                out_specs=self.state_spec(),
                scratch_shapes=[
                    pltpu.VMEM((lay.spread, HEAD), jnp.bfloat16),
                    pltpu.VMEM((lay.spread, HEAD), jnp.bfloat16),
                    pltpu.VMEM((lay.mem_spread, lay.unit), jnp.bfloat16),
                ],
            ),
            out_shape=jax.ShapeDtypeStruct((lay.groups, STATE_ROWS, HEAD), jnp.float32),
            compiler_params=pltpu.CompilerParams(vmem_limit_bytes=VMEM_LIMIT),
            cost_estimate=SMALL,
            name="memory_write",
        )(self.places, *self.slots)

    def attend(self, state, block=0, blocks=1, begun=()):
        lay = self.lay
        out_spec = pl.BlockSpec((lay.stride, lay.wide), lambda i, *_: (0, block))
        return list(
            pl.pallas_call(
                functools.partial(token_kernel, lay, len(begun)),
                grid_spec=pltpu.PrefetchScalarGridSpec(
                    num_scalar_prefetch=1,
                    grid=(1,),
                    in_specs=self.slot_specs()
                    + [self.state_spec()]
                    + [pl.BlockSpec(memory_space=pl.ANY)] * len(begun),
                    out_specs=[out_spec] * lay.slots,
                    scratch_shapes=[
                        pltpu.VMEM((lay.spread, lay.wide), jnp.bfloat16),
                        pltpu.VMEM((lay.full, HEAD), jnp.bfloat16),
                        pltpu.VMEM((lay.full, HEAD), jnp.bfloat16),
                        pltpu.VMEM((lay.spread, lay.wide), jnp.float32),
                    ],
                ),
                out_shape=[jax.ShapeDtypeStruct((lay.stride, blocks * lay.wide), jnp.bfloat16)]
                * lay.slots,
                input_output_aliases={2 + lay.slots + i: i for i in range(len(begun))},
                compiler_params=pltpu.CompilerParams(vmem_limit_bytes=VMEM_LIMIT),
                cost_estimate=SMALL,
                name="token_attention",
            )(self.places, *self.slots, state, *begun)
        )


def relay(writes, rates, works):
    size = lax.axis_size("seg")
    me = lax.axis_index("seg")
    ids = lax.broadcasted_iota(jnp.int32, (size, 1), 0)

    def product(mask):
        return jnp.prod(jnp.where(mask, rates, 1.0), axis=0)[:, None, None]

    total = writes
    prefix = jnp.zeros_like(writes)
    results = []
    bit = 1
    while bit < size:
        route = [(i, i ^ bit) for i in range(size)]
        sent = total.astype(jnp.bfloat16)
        got = lax.ppermute(sent, "seg", route)
        if len(results) < len(works):
            results.append(works[len(results)](sent))
            got = tie(got, results[-1])
        got = got.astype(jnp.float32)
        mine = ids // bit == me // bit
        theirs = ids // bit == (me // bit) ^ 1
        upper = (me // bit) % 2 == 1
        prefix = jnp.where(upper, product(mine & (ids < me)) * got + prefix, prefix)
        total = jnp.where(upper, product(mine) * got + total, product(theirs) * total + got)
        bit *= 2
    for work in works[len(results) :]:
        results.append(work(prefix))
    return prefix, results


def output_kernel(plan, bufs, picks, final, ids_ref, mixed_ref, other_ref, own_ref, *refs):
    count = 1 + max(p for row in plan for parts in row if parts is not None for p in parts)
    piece_refs, refs = refs[:count], refs[count:]
    if final:
        base_ref, begun_ref, out_ref, far_ref, weights, total, sems = refs
    else:
        out_ref, weights, total, sems = refs
    rows = mixed_ref.shape[1]
    blocks, groups = len(plan), len(plan[0])
    width = weights.shape[2]
    c, g = pl.program_id(0), pl.program_id(1)
    step = c * groups + g
    steps = blocks * groups

    def start(at):
        slot = lax.rem(at, bufs)
        for b in range(blocks):
            for j in range(groups):

                @pl.when(at == b * groups + j)
                def _():
                    if plan[b][j] is None:
                        columns = pl.ds(pl.multiple_of(ids_ref[b] * width, 128), width)
                        pltpu.make_async_copy(
                            own_ref.at[:, columns], weights.at[slot], sems.at[slot]
                        ).start()
                        return
                    row = 0
                    for index in plan[b][j]:
                        part = piece_refs[index]
                        high = part.shape[0]
                        pltpu.make_async_copy(
                            part, weights.at[slot, pl.ds(row, high), :], sems.at[slot]
                        ).start()
                        row += high

    @pl.when(step == 0)
    def _():
        for at in range(min(bufs - 1, steps)):
            start(jnp.int32(at))

    @pl.when(step + bufs - 1 < steps)
    def _():
        start(step + bufs - 1)

    slot = lax.rem(step, bufs)
    pltpu.make_async_copy(weights.at[slot], weights.at[slot], sems.at[slot]).wait()
    both = jnp.concatenate([mixed_ref[picks + g], other_ref[picks + g]], axis=0)
    term = jnp.dot(both, weights[slot], preferred_element_type=jnp.float32)

    @pl.when(g == 0)
    def _():
        total[...] = term + begun_ref[0] if final else term

    @pl.when(g > 0)
    def _():
        total[...] = total[...] + term

    @pl.when(g == groups - 1)
    def _():
        if final:
            base = base_ref[...].astype(jnp.float32)
            out_ref[...] = (base + total[:rows, :]).astype(out_ref.dtype)
            far_ref[...] = total[rows:, :].astype(far_ref.dtype)
        else:
            out_ref[0] = total[...]


def output_product(mixed, other, tokens, w_out, gathered, begun=None):
    count, rows, depth = mixed.shape
    final = begun is not None
    blocks = len(gathered[0])
    width = w_out.shape[1] // (2 * blocks)
    chips = jnp.stack([gathered[0][b][1] for b in range(blocks)]).astype(jnp.int32)
    ids = (lax.axis_index("seg") % 2) * blocks + chips
    plan, pieces = [], []
    for b in range(blocks):
        row = [] if final else [None]
        for pieces_of in gathered:
            parts = pieces_of[b][0]
            row.append(tuple(range(len(pieces), len(pieces) + len(parts))))
            pieces += parts
        plan.append(row)
    groups = len(plan[0])
    picks = count - groups if final else 0
    bufs = 4
    whole = pl.BlockSpec((rows, width), lambda c, g, ids: (0, ids[c]))
    half = pl.BlockSpec((rows, width), lambda c, g, ids: (0, lax.rem(ids[c], blocks)))
    sums = pl.BlockSpec((1, 2 * rows, width), lambda c, g, ids: (c, 0, 0))
    mixed_spec = pl.BlockSpec((count, rows, depth), lambda c, g, ids: (0, 0, 0))
    if final:
        shapes = [
            jax.ShapeDtypeStruct((rows, w_out.shape[1]), jnp.bfloat16),
            jax.ShapeDtypeStruct((rows, w_out.shape[1] // 2), jnp.bfloat16),
        ]
    else:
        shapes = jax.ShapeDtypeStruct((blocks, 2 * rows, width), jnp.float32)
    return pl.pallas_call(
        functools.partial(output_kernel, plan, bufs, picks, final),
        grid_spec=pltpu.PrefetchScalarGridSpec(
            num_scalar_prefetch=1,
            grid=(blocks, groups),
            in_specs=[mixed_spec] * 2
            + [pl.BlockSpec(memory_space=pl.ANY)] * (1 + len(pieces))
            + ([whole, sums] if final else []),
            out_specs=[whole, half] if final else sums,
            scratch_shapes=[
                pltpu.VMEM((bufs, depth, width), jnp.bfloat16),
                pltpu.VMEM((2 * rows, width), jnp.float32),
                pltpu.SemaphoreType.DMA((bufs,)),
            ],
        ),
        out_shape=shapes,
        compiler_params=pltpu.CompilerParams(vmem_limit_bytes=VMEM_LIMIT),
        cost_estimate=SMALL,
        name="output_product",
    )(ids, mixed, other, w_out, *pieces, *((tokens, begun) if final else ()))


def project_kernel(heights, parts, kv_heads, *refs):
    pieces = [ref for ref in refs[: sum(map(len, heights))]]
    refs = refs[len(pieces) :]
    weights, outs = refs[:parts], refs[parts : parts + len(heights)]
    totals = refs[parts + len(heights) :]
    step, steps = pl.program_id(0), pl.num_programs(0)
    x = [ref[...] for ref in pieces]
    x = x[0] if len(x) == 1 else jnp.concatenate(x, axis=0)
    for weight, total in zip(weights, totals):
        term = jnp.dot(x, weight[...], preferred_element_type=jnp.float32)

        @pl.when(step == 0)
        def _():
            total[...] = term

        @pl.when(step > 0)
        def _():
            total[...] = total[...] + term

    @pl.when(step == steps - 1)
    def _():
        height = sum(heights[0])
        for i, out in enumerate(outs):
            rows = slice(i * height, (i + 1) * height)
            start = 0
            for h in range(kv_heads):
                for total in totals:
                    width = total.shape[1] // kv_heads
                    part = total[rows, h * width : (h + 1) * width]
                    out[:, start : start + width] = part.astype(out.dtype)
                    start += width


def project(slots, weights, kv_heads=1):
    heights = [[x.shape[0] for x in slot] for slot in slots]
    depth = slots[0][0].shape[1]
    block = depth // 8
    widths = [w.shape[1] for w in weights]
    shape = jax.ShapeDtypeStruct((sum(heights[0]), sum(widths)), jnp.bfloat16)
    rows = sum(map(sum, heights))
    return list(
        pl.pallas_call(
            functools.partial(project_kernel, heights, len(weights), kv_heads),
            grid=(depth // block,),
            in_specs=[pl.BlockSpec((h, block), lambda k: (0, k)) for hs in heights for h in hs]
            + [pl.BlockSpec((block, width), lambda k: (k, 0)) for width in widths],
            out_specs=[pl.BlockSpec(shape.shape, lambda k: (0, 0))] * len(slots),
            out_shape=[shape] * len(slots),
            scratch_shapes=[pltpu.VMEM((rows, w), jnp.float32) for w in widths],
            compiler_params=pltpu.CompilerParams(vmem_limit_bytes=VMEM_LIMIT),
            cost_estimate=SMALL,
            name="project",
        )(*sum(map(list, slots), []), *weights)
    )


def per_device(tokens, memory_embed, norm_gain, w_query, w_key, value_weight, w_out, retain):
    planes = Planes(lax.axis_size("tensor"))
    turns = list(planes.turns)
    me = lax.axis_index("tensor")
    seg, seg_count = lax.axis_index("seg"), lax.axis_size("seg")
    core, chip, chips = seg % 2, seg // 2, seg_count // 2
    is_end = (me < planes.quarter) | (me >= 3 * planes.quarter)
    worker = jnp.where(is_end, planes.partner(me), me)
    heads, kv_heads = w_query.shape[1] // HEAD, w_key.shape[1] // HEAD
    groups = heads // kv_heads
    lay = Layout(planes.count, tokens.shape[0], memory_embed.shape[0], groups)
    back, lend = planes.give_back(), planes.lend()

    depth = w_query.shape[0] // seg_count

    lent_shares = []
    for h in range(kv_heads):
        cuts = []
        for array, wide in ((w_query, lay.wide), (w_key, HEAD), (value_weight, HEAD)):
            cuts.append(lax.dynamic_slice(array, (seg * depth, h * wide), (depth, wide)))
        lent_shares.append(jnp.concatenate(cuts, axis=1))
    half = w_out.shape[1] // 2
    width = half // chips
    share = lax.dynamic_slice_in_dim(w_out, core * half + chip * width, width, 1)

    places = [me, planes.partner(me)]
    for turn in turns:
        peer = planes.peer(worker, turn)
        places += [peer, planes.partner(peer)]
    places = jnp.stack(places).astype(jnp.int32)
    own_weights = [w_query, w_key, value_weight]
    numbers = [0, 1] + [2 + 2 * at for at in range(len(turns))]
    far_numbers = [3 + 2 * at for at in range(len(turns))]
    half_rows = lay.height // 2
    own, taken = {}, [{} for _ in range(kv_heads)]

    lent = [hop(lent_shares[0], lend)]
    peers = [hop(share, planes.exchange(turn)) for turn in turns]
    near_back = hop(share, back)
    rates = jnp.concatenate([retain, hop(retain, lend)], axis=1)
    gain = tie(norm_gain, share, lent_shares)
    rows = jnp.concatenate(
        [pad_rows(rms_rows(tokens, gain)), pad_rows(rms_rows(memory_embed, gain))], axis=0
    )
    lent, peers, near_back, rows, share, lent_shares, rates = gate(
        lent, peers, near_back, rows, share, lent_shares, rates
    )

    lent_all = [lax.all_gather(lent[0], "seg", axis=0, tiled=True)]
    rows_a = hop(rows, lend)
    near_rows = [hop(rows, planes.exchange(turn)) for turn in turns]
    rings = [ChipRing(jnp.where(is_end, near_back, peers[0]))]
    (own[0],) = project([[rows]], own_weights, kv_heads)
    rates = seg_all(tie(rates, own[0]))
    held = (rings[0].right, rings[0].left)
    rows_a, near_rows, held, own, rows, share, lent_shares, peers, rates = gate(
        rows_a, near_rows, held, own, rows, share, lent_shares, peers, rates
    )
    rings[0].right, rings[0].left = held

    lent += [hop(part, lend) for part in lent_shares[1:]]
    far_rows = [[hop(rows_a[:half_rows], planes.exchange(turn))] for turn in turns]
    ends = [hop(piece, back) for piece in peers]
    closed = rings[0].close()
    known = [[rows], [rows_a]] + [[x] for x in near_rows]
    own.update(zip(numbers[1:], project(known[1:], own_weights, kv_heads)))
    lent, far_rows, ends, rings[0].last, own, known, lent_all, share, rows_a = gate(
        lent, far_rows, ends, closed, own, known, lent_all, share, rows_a
    )

    lent_all += [lax.all_gather(part, "seg", axis=0, tiled=True) for part in lent[1:]]
    for parts, turn in zip(far_rows, turns):
        parts.append(hop(rows_a[half_rows:], planes.exchange(turn)))
    near = hop(share, lend)
    taken[0].update(zip(numbers, project(known, [lent_all[0]])))
    far_rows, near, taken, known, ends = gate(far_rows, near, taken, known, ends)

    far_near = [hop(near, planes.exchange(turn)) for turn in turns]
    for end, mid in zip(ends, peers[1:] + [near]):
        rings.append(ChipRing(jnp.where(is_end, end, mid)))
    own.update(zip(far_numbers, project(far_rows, own_weights, kv_heads)))
    order = range(planes.count)
    own_slots = [own[slot] for slot in order]
    own_units = [Unit(lay, places, own_slots, h) for h in range(kv_heads)]
    writes = jnp.concatenate([u.memory_write() for u in own_units], axis=0)

    def first_lent(dep):
        taken[0].update(zip(far_numbers, project([tie(x, dep) for x in far_rows], [lent_all[0]])))
        return taken[0][far_numbers[-1]]

    def other_lent(dep, h):
        part = tie(lent_all[h], dep)
        taken[h].update(zip(numbers + far_numbers, project(known + far_rows, [part])))
        return taken[h][far_numbers[-1]]

    works = [first_lent]
    works += [functools.partial(other_lent, h=h) for h in range(1, kv_heads)]
    state, _ = relay(writes, rates[:, :heads], works)

    held = [(ring.right, ring.left) for ring in rings[1:]]
    far_near, own_slots, taken, held, state = gate(far_near, own_slots, taken, held, state)
    for ring, (right, left) in zip(rings[1:], held):
        ring.right, ring.left = right, left
        ring.close()
    backs = [hop(piece, back) for piece in far_near]
    own_units = [Unit(lay, places, own_slots, h) for h in range(kv_heads)]
    lent_units = [Unit(lay, places, [part[slot] for slot in order]) for part in taken]
    writes = jnp.concatenate([u.memory_write() for u in lent_units], axis=0)
    mixed_own = []

    def attend_own(dep, h):
        unit = own_units[h].tied(dep)
        mixed_own[:] = unit.attend(state[h * groups : (h + 1) * groups], h, kv_heads, mixed_own)
        return mixed_own

    works = [functools.partial(attend_own, h=h) for h in range(kv_heads)]
    lent_state, _ = relay(writes, rates[:, heads:], works)

    last = rings[-1].last
    lent_state, mixed_own, backs, last = gate(lent_state, list(mixed_own), backs, last)
    rings[-1].last = last
    late = len(rings)
    for mid, end in zip(far_near, backs):
        rings.append(ChipRing(tie(jnp.where(is_end, end, mid), last)))

    def cross(arrays):
        return (
            arrays[0],
            hop(arrays[1], back),
            [hop(arrays[2 + 2 * at], planes.exchange(turn)) for at, turn in enumerate(turns)],
            [hop(arrays[3 + 2 * at], planes.far_back(turn)) for at, turn in enumerate(turns)],
        )

    crossed = [cross(mixed_own)]
    for h, unit in enumerate(lent_units):
        crossed.append(cross(unit.tied(lent_state).attend(lent_state[h * groups : (h + 1) * groups])))

    def join(arrays):
        both = jnp.concatenate(arrays, axis=1)
        return both[:, : heads * HEAD], both[:, heads * HEAD :]

    home = join([c[0] for c in crossed])
    returned = join([c[1] for c in crossed])
    near_mixed = [join([c[2][at] for c in crossed]) for at in range(len(turns))]
    far_mixed = [join([c[3][at] for c in crossed]) for at in range(len(turns))]
    ends = [returned[1], returned[0]] + [m[0] for m in far_mixed] + [m[1] for m in far_mixed]
    mids = [home[0]] + [m[0] for m in near_mixed] + [home[1]] + [m[1] for m in near_mixed]
    mixed = jnp.stack([jnp.where(is_end, e, m) for e, m in zip(ends, mids)])

    held = [(ring.right, ring.left) for ring in rings[late:]]
    mixed, held = gate(mixed, held)
    for ring, (right, left) in zip(rings[late:], held):
        ring.right, ring.left = right, left
        ring.close()
    gathered = [ring.pieces() for ring in rings]
    other = swap_cores(mixed)
    base = pad_rows(tokens)
    begun = output_product(mixed, other, base, w_out, gathered[:late])
    result, other = output_product(mixed, other, base, w_out, gathered[late:], begun)
    other = swap_cores(other)
    start = (1 - core) * half
    base = lax.dynamic_slice_in_dim(base, start, half, 1)
    other = (base.astype(jnp.float32) + other.astype(jnp.float32)).astype(jnp.bfloat16)
    result = lax.dynamic_update_slice_in_dim(result, other, start, 1)
    return result[: tokens.shape[0]]


def solution(mesh):
    return jax.shard_map(
        per_device,
        mesh=mesh,
        in_specs=(
            P(("seg", "tensor"), None),
            P("tensor", None),
            P(),
            P(None, "tensor"),
            P(None, "tensor"),
            P(None, "tensor"),
            P("tensor", None),
            P("seg", "tensor"),
        ),
        out_specs=P(("seg", "tensor"), None),
        check_vma=False,
    )
```

```python
import functools

import jax
import jax.numpy as jnp
from jax import lax
from jax.experimental import pallas as pl
from jax.experimental.pallas import tpu as pltpu
from jax.sharding import PartitionSpec as P

HEAD = 128
EPSILON = 1e-05
SCALE = HEAD ** (-0.5)
LOG2E = 1.4426950408889634
STATE_ROWS = HEAD + 16
VMEM_LIMIT = 48 * 1024 * 1024
SMALL = pl.CostEstimate(flops=1, bytes_accessed=1, transcendentals=0)


def rms_rows(rows, norm_gain):
    widened = rows.astype(jnp.float32)
    scale_rows = lax.rsqrt(jnp.mean(widened * widened, axis=-1, keepdims=True) + EPSILON)
    return (widened * scale_rows * norm_gain.astype(jnp.float32)).astype(jnp.bfloat16)


def feature_map(inputs):
    return jnp.exp(jnp.minimum(inputs, 0.0)) + jnp.maximum(inputs, 0.0)


def tie(value, *others):
    return lax.optimization_barrier((value,) + others)[0]


def gate(*values):
    return lax.optimization_barrier(values)


class Planes:
    def __init__(self, count):
        self.count = count
        self.quarter = count // 4
        self.workers = range(self.quarter, 3 * self.quarter)
        self.ends = [i for i in range(count) if i not in self.workers]
        self.turns = range(1, count // 2)

    def partner(self, index):
        return index ^ self.quarter

    def peer(self, index, turn):
        return self.quarter + ((index - self.quarter) ^ turn)

    def lend(self):
        return [(e, self.partner(e)) for e in self.ends]

    def give_back(self):
        return [(w, self.partner(w)) for w in self.workers]

    def pairs(self):
        return [(i, self.partner(i)) for i in range(self.count)]

    def exchange(self, turn):
        return [(w, self.peer(w, turn)) for w in self.workers]

    def far_back(self, turn):
        return [(w, self.partner(self.peer(w, turn))) for w in self.workers]


def hop(block, pairs):
    return lax.ppermute(block, "tensor", pairs)


def seg_cycle(chips):
    half = chips // 2
    return list(range(half)) + list(range(chips - 1, half - 1, -1))


def swap_cores(block):
    return lax.ppermute(block, "seg", [(i, i ^ 1) for i in range(lax.axis_size("seg"))])


def ring_order():
    chips = lax.axis_size("seg") // 2
    cycle = seg_cycle(chips)
    place_of = [cycle.index(c) for c in range(chips)]
    place = jnp.array(place_of, jnp.int32)[lax.axis_index("seg") // 2]
    steps = [0] + [s for turn in range(1, chips // 2) for s in (-turn, turn)] + [chips // 2]
    return jnp.array(cycle, jnp.int32)[(place + jnp.array(steps) + chips) % chips]


class ChipRing:
    def __init__(self, block, straight=False):
        self.chips = lax.axis_size("seg") // 2
        self.cycle = seg_cycle(self.chips)
        self.block, self.right, self.left, self.last = block, [block], [block], None
        for _ in range(1, self.chips // 2):
            self.right.append(self.step(self.right[-1], 1))
            self.left.append(self.step(self.left[-1], -1))
        if straight:
            self.last = (self.step(block, self.chips // 2),)

    def step(self, part, distance):
        route = [
            (self.cycle[i] * 2 + c, self.cycle[(i + distance) % self.chips] * 2 + c)
            for i in range(self.chips)
            for c in range(2)
        ]
        return lax.ppermute(part, "seg", route)

    def halves(self):
        half = self.block.shape[0] // 2
        return self.right[-1][:half], self.left[-1][half:]

    def close(self, halves=None):
        right, left = halves or self.halves()
        self.last = (self.step(right, 1), self.step(left, -1))

    def pieces(self):
        found = [(self.block,)]
        for turn in range(1, self.chips // 2):
            found += [(self.right[turn],), (self.left[turn],)]
        return found + [self.last]


def seg_double(values, bit):
    size = lax.axis_size("seg")
    got = lax.ppermute(values, "seg", [(i, i ^ bit) for i in range(size)])
    upper = (lax.axis_index("seg") // bit) % 2 == 1
    return jnp.concatenate(
        [jnp.where(upper, got, values), jnp.where(upper, values, got)], axis=0
    )


def pad_to(value, unit):
    return -(-value // unit) * unit


def pad_rows(array, unit=16):
    return jnp.pad(array, ((0, pad_to(array.shape[0], unit) - array.shape[0]), (0, 0)))


def nt_dot(a, b):
    return lax.dot_general(a, b, (((1,), (1,)), ((), ())), preferred_element_type=jnp.float32)


class Layout:
    def __init__(self, slots, rows, mem, groups):
        self.slots, self.rows, self.mem, self.groups = slots, rows, mem, groups
        self.stride, self.mem_stride = pad_to(rows, 16), pad_to(mem, 16)
        self.height = self.stride + self.mem_stride
        self.spread = slots * self.stride
        self.mem_spread = slots * self.mem_stride
        self.full = pad_to(self.spread, 128)
        self.wide = groups * HEAD
        self.unit = (groups + 2) * HEAD

    def valid(self, ids):
        return lax.rem(ids, self.stride) < self.rows

    def mem_valid(self, ids):
        return lax.rem(ids, self.mem_stride) < self.mem


def memory_kernel(lay, place_ref, *refs):
    slots, out_ref, key_all, value_all, mem_all = refs[: lay.slots], *refs[lay.slots :]
    wide = lay.wide
    for i, ref in enumerate(slots):
        start = pl.multiple_of(place_ref[i] * lay.stride, 16)
        key_all[pl.ds(start, lay.stride), :] = ref[: lay.stride, wide : wide + HEAD]
        value_all[pl.ds(start, lay.stride), :] = ref[: lay.stride, wide + HEAD :]
        start = pl.multiple_of(place_ref[i] * lay.mem_stride, 16)
        mem_all[pl.ds(start, lay.mem_stride), :] = ref[lay.stride :, :]
    k_tok, v_tok = key_all[...], value_all[...]
    k_mem, v_mem = mem_all[:, wide : wide + HEAD], mem_all[:, wide + HEAD :]
    mem = lay.mem_spread
    row_ids = lax.broadcasted_iota(jnp.int32, (mem, mem), 0)
    col_ids = lax.broadcasted_iota(jnp.int32, (mem, mem), 1)
    keep = row_ids >= col_ids
    feat = feature_map(k_mem.astype(jnp.float32))
    if lay.mem_stride != lay.mem:
        keep = keep & lay.mem_valid(col_ids)
        feat_ids = lax.broadcasted_iota(jnp.int32, (mem, HEAD), 0)
        feat = jnp.where(lay.mem_valid(feat_ids), feat, 0.0)
    feat_sum = jnp.sum(feat, axis=0, keepdims=True)
    feat_cast = feat.astype(jnp.bfloat16)
    for g in range(lay.groups):
        q = mem_all[:, g * HEAD : (g + 1) * HEAD]
        s_tok = nt_dot(q, k_tok)
        if lay.stride != lay.rows:
            ids = lax.broadcasted_iota(jnp.int32, (mem, lay.spread), 1)
            s_tok = jnp.where(lay.valid(ids), s_tok, -1e30)
        s_mem = jnp.where(keep, nt_dot(q, k_mem), -1e30)
        top = jnp.maximum(
            jnp.max(s_tok, axis=1, keepdims=True), jnp.max(s_mem, axis=1, keepdims=True)
        )
        p_tok = jnp.exp2((s_tok - top) * (SCALE * LOG2E))
        p_mem = jnp.exp2((s_mem - top) * (SCALE * LOG2E))
        total = jnp.sum(p_tok, axis=1, keepdims=True) + jnp.sum(p_mem, axis=1, keepdims=True)
        soft = jnp.dot(
            p_tok.astype(jnp.bfloat16), v_tok, preferred_element_type=jnp.float32
        ) + jnp.dot(p_mem.astype(jnp.bfloat16), v_mem, preferred_element_type=jnp.float32)
        soft = soft / total
        out_ref[g, :HEAD, :] = lax.dot_general(
            feat_cast,
            soft.astype(jnp.bfloat16),
            (((0,), (0,)), ((), ())),
            preferred_element_type=jnp.float32,
        )
        out_ref[g, HEAD:, :] = jnp.broadcast_to(feat_sum, (STATE_ROWS - HEAD, HEAD))


def read_state(query, state, sums):
    feat = feature_map(query.astype(jnp.float32)).astype(jnp.bfloat16)
    numerator = jnp.dot(feat, state.astype(jnp.bfloat16), preferred_element_type=jnp.float32)
    sums = jnp.broadcast_to(sums, (HEAD, HEAD)).astype(jnp.bfloat16)
    return numerator / (nt_dot(feat, sums) + 1.0)


def token_kernel(lay, first_head, heads, begun, place_ref, *refs):
    count, stride, wide = lay.slots, lay.stride, lay.wide
    slots, refs = refs[:count], refs[count:]
    state_ref, refs = refs[0], refs[1 + begun :]
    outs, (query_all, key_all, value_all, out_all) = refs[:count], refs[count:]
    if lay.full > lay.spread:
        tail = (lay.full - lay.spread, HEAD)
        key_all[lay.spread :, :] = jnp.zeros(tail, key_all.dtype)
        value_all[lay.spread :, :] = jnp.zeros(tail, value_all.dtype)
    for i, ref in enumerate(slots):
        rows = pl.ds(pl.multiple_of(place_ref[i] * stride, 16), stride)
        query_all[rows, :] = ref[:stride, first_head * HEAD : (first_head + heads) * HEAD]
        key_all[rows, :] = ref[:stride, wide : wide + HEAD]
        value_all[rows, :] = ref[:stride, wide + HEAD :]

    for block in range(count):
        first = block * stride
        low = first // 128 * 128
        high = min(pad_to(first + stride, 128), lay.full)
        k_diag, v_diag = key_all[low:high, :], value_all[low:high, :]
        row_ids = lax.broadcasted_iota(jnp.int32, (stride, high - low), 0) + first
        col_ids = lax.broadcasted_iota(jnp.int32, (stride, high - low), 1) + low
        keep = row_ids >= col_ids
        if stride != lay.rows:
            keep = keep & lay.valid(col_ids)

        def one_head(g, carry, first=first, low=low, k_diag=k_diag, v_diag=v_diag, keep=keep):
            lanes = pl.ds(pl.multiple_of(g * HEAD, HEAD), HEAD)
            q = query_all[first : first + stride, lanes]
            at = first_head + g
            s_diag = jnp.where(keep, nt_dot(q, k_diag), -1e30)
            top = jnp.max(s_diag, axis=1, keepdims=True)
            if low > 0:
                s_prev = nt_dot(q, key_all[:low, :])
                if stride != lay.rows:
                    ids = lax.broadcasted_iota(jnp.int32, (stride, low), 1)
                    s_prev = jnp.where(lay.valid(ids), s_prev, -1e30)
                top = jnp.maximum(top, jnp.max(s_prev, axis=1, keepdims=True))
            p_diag = jnp.exp2((s_diag - top) * (SCALE * LOG2E))
            total = jnp.sum(p_diag, axis=1, keepdims=True)
            soft = jnp.dot(
                p_diag.astype(jnp.bfloat16), v_diag, preferred_element_type=jnp.float32
            )
            if low > 0:
                p_prev = jnp.exp2((s_prev - top) * (SCALE * LOG2E))
                total = total + jnp.sum(p_prev, axis=1, keepdims=True)
                soft = soft + jnp.dot(
                    p_prev.astype(jnp.bfloat16),
                    value_all[:low, :],
                    preferred_element_type=jnp.float32,
                )
            state, sums = state_ref[at, :HEAD, :], state_ref[at, HEAD : HEAD + 1, :]
            out_all[first : first + stride, lanes] = soft / total + read_state(q, state, sums)
            return carry

        lax.fori_loop(0, heads, one_head, 0)

    for i, ref in enumerate(outs):
        rows = pl.ds(pl.multiple_of(place_ref[i] * stride, 16), stride)
        ref[...] = out_all[rows, :].astype(ref.dtype)


class Unit:
    def __init__(self, lay, places, slots, at=0):
        self.lay, self.places, self.slots, self.at = lay, places, slots, at

    def tied(self, *others):
        return Unit(self.lay, self.places, [tie(s, *others) for s in self.slots], self.at)

    def slot_specs(self):
        lay, at = self.lay, self.at
        return [pl.BlockSpec((lay.height, lay.unit), lambda i, *_: (0, at))] * lay.slots

    def state_spec(self):
        return pl.BlockSpec((self.lay.groups, STATE_ROWS, HEAD), lambda i, *_: (0, 0, 0))

    def memory_write(self):
        lay = self.lay
        return pl.pallas_call(
            functools.partial(memory_kernel, lay),
            grid_spec=pltpu.PrefetchScalarGridSpec(
                num_scalar_prefetch=1,
                grid=(1,),
                in_specs=self.slot_specs(),
                out_specs=self.state_spec(),
                scratch_shapes=[
                    pltpu.VMEM((lay.spread, HEAD), jnp.bfloat16),
                    pltpu.VMEM((lay.spread, HEAD), jnp.bfloat16),
                    pltpu.VMEM((lay.mem_spread, lay.unit), jnp.bfloat16),
                ],
            ),
            out_shape=jax.ShapeDtypeStruct((lay.groups, STATE_ROWS, HEAD), jnp.float32),
            compiler_params=pltpu.CompilerParams(vmem_limit_bytes=VMEM_LIMIT),
            cost_estimate=SMALL,
            name="memory_write",
        )(self.places, *self.slots)

    def attend(self, state, first_head=0, heads=None, block=0, blocks=1, begun=()):
        lay = self.lay
        heads = heads or lay.groups
        wide = heads * HEAD
        out_spec = pl.BlockSpec((lay.stride, wide), lambda i, *_: (0, block))
        return list(
            pl.pallas_call(
                functools.partial(token_kernel, lay, first_head, heads, len(begun)),
                grid_spec=pltpu.PrefetchScalarGridSpec(
                    num_scalar_prefetch=1,
                    grid=(1,),
                    in_specs=self.slot_specs()
                    + [self.state_spec()]
                    + [pl.BlockSpec(memory_space=pl.ANY)] * len(begun),
                    out_specs=[out_spec] * lay.slots,
                    scratch_shapes=[
                        pltpu.VMEM((lay.spread, wide), jnp.bfloat16),
                        pltpu.VMEM((lay.full, HEAD), jnp.bfloat16),
                        pltpu.VMEM((lay.full, HEAD), jnp.bfloat16),
                        pltpu.VMEM((lay.spread, wide), jnp.float32),
                    ],
                ),
                out_shape=[jax.ShapeDtypeStruct((lay.stride, blocks * wide), jnp.bfloat16)]
                * lay.slots,
                input_output_aliases={2 + lay.slots + i: i for i in range(len(begun))},
                compiler_params=pltpu.CompilerParams(vmem_limit_bytes=VMEM_LIMIT),
                cost_estimate=SMALL,
                name="token_attention",
            )(self.places, *self.slots, state, *begun)
        )


def relay(writes, rates, works):
    size = lax.axis_size("seg")
    me = lax.axis_index("seg")
    ids = lax.broadcasted_iota(jnp.int32, (size, 1), 0)

    def product(mask):
        return jnp.prod(jnp.where(mask, rates, 1.0), axis=0)[:, None, None]

    total = writes
    prefix = jnp.zeros_like(writes)
    results = []
    bit = 1
    while bit < size:
        route = [(i, i ^ bit) for i in range(size)]
        sent = total.astype(jnp.bfloat16)
        got = lax.ppermute(sent, "seg", route)
        if len(results) < len(works):
            results.append(works[len(results)](sent))
            got = tie(got, results[-1])
        got = got.astype(jnp.float32)
        mine = ids // bit == me // bit
        theirs = ids // bit == (me // bit) ^ 1
        upper = (me // bit) % 2 == 1
        prefix = jnp.where(upper, product(mine & (ids < me)) * got + prefix, prefix)
        total = jnp.where(upper, product(mine) * got + total, product(theirs) * total + got)
        bit *= 2
    for work in works[len(results) :]:
        results.append(work(prefix))
    return prefix, results


def output_kernel(plan, low, final, ids_ref, mixed_ref, other_ref, own_ref, *refs):
    count = 1 + max(p for row in plan for p in row if p is not None)
    piece_refs, refs = refs[:count], refs[count:]
    if final:
        base_ref, begun_ref, out_ref, far_ref, both, weights, sems = refs
    else:
        out_ref, both, weights, sems = refs
    rows = mixed_ref.shape[0]
    blocks = len(plan)
    _, depth, width = weights.shape
    step = pl.program_id(0)

    def start(at):
        slot = lax.rem(at, 2)
        for b in range(blocks):

            @pl.when(at == b)
            def _():
                row = 0
                for index in plan[b]:
                    if index is None:
                        columns = pl.ds(pl.multiple_of(ids_ref[b] * width, 128), width)
                        part = own_ref.at[:, columns]
                    else:
                        part = piece_refs[index]
                    high = part.shape[0]
                    pltpu.make_async_copy(
                        part, weights.at[slot, pl.ds(row, high), :], sems.at[slot]
                    ).start()
                    row += high

    @pl.when(step == 0)
    def _():
        start(jnp.int32(0))
        both[:rows, :] = mixed_ref[:, low : low + depth]
        both[rows:, :] = other_ref[:, low : low + depth]

    @pl.when(step + 1 < blocks)
    def _():
        start(step + 1)

    slot = lax.rem(step, 2)
    pltpu.make_async_copy(weights.at[slot], weights.at[slot], sems.at[slot]).wait()
    term = jnp.dot(both[...], weights[slot], preferred_element_type=jnp.float32)
    if final:
        term = term + begun_ref[0].astype(jnp.float32)
        base = base_ref[...].astype(jnp.float32)
        out_ref[...] = (base + term[:rows, :]).astype(out_ref.dtype)
        far_ref[...] = term[rows:, :].astype(far_ref.dtype)
    else:
        out_ref[0] = term.astype(out_ref.dtype)


def output_product(mixed, other, tokens, w_out, ids, gathered, begun=None):
    rows = mixed.shape[0]
    final = begun is not None
    blocks = len(gathered[0])
    width = w_out.shape[1] // (2 * blocks)
    plan, pieces = [], []
    for b in range(blocks):
        row = [] if final else [None]
        for parts in gathered:
            row += range(len(pieces), len(pieces) + len(parts[b]))
            pieces += parts[b]
        plan.append(row)
    depth = w_out.shape[0] * (len(gathered) + (0 if final else 1))
    low = mixed.shape[1] - depth if final else 0
    whole = pl.BlockSpec((rows, width), lambda c, ids: (0, ids[c]))
    half = pl.BlockSpec((rows, width), lambda c, ids: (0, lax.rem(ids[c], blocks)))
    sums = pl.BlockSpec((1, 2 * rows, width), lambda c, ids: (c, 0, 0))
    mixed_spec = pl.BlockSpec(mixed.shape, lambda c, ids: (0, 0))
    if final:
        shapes = [
            jax.ShapeDtypeStruct((rows, w_out.shape[1]), jnp.bfloat16),
            jax.ShapeDtypeStruct((rows, w_out.shape[1] // 2), jnp.bfloat16),
        ]
    else:
        shapes = jax.ShapeDtypeStruct((blocks, 2 * rows, width), jnp.bfloat16)
    return pl.pallas_call(
        functools.partial(output_kernel, plan, low, final),
        grid_spec=pltpu.PrefetchScalarGridSpec(
            num_scalar_prefetch=1,
            grid=(blocks,),
            in_specs=[mixed_spec] * 2
            + [pl.BlockSpec(memory_space=pl.ANY)] * (1 + len(pieces))
            + ([whole, sums] if final else []),
            out_specs=[whole, half] if final else sums,
            scratch_shapes=[
                pltpu.VMEM((2 * rows, depth), jnp.bfloat16),
                pltpu.VMEM((2, depth, width), jnp.bfloat16),
                pltpu.SemaphoreType.DMA((2,)),
            ],
        ),
        out_shape=shapes,
        compiler_params=pltpu.CompilerParams(vmem_limit_bytes=VMEM_LIMIT),
        cost_estimate=SMALL,
        name="output_product",
    )(ids, mixed, other, w_out, *pieces, *((tokens, begun) if final else ()))


def project_kernel(heights, parts, kv_heads, *refs):
    pieces = [ref for ref in refs[: sum(map(len, heights))]]
    refs = refs[len(pieces) :]
    weights, outs = refs[:parts], refs[parts : parts + len(heights)]
    totals = refs[parts + len(heights) :]
    step, steps = pl.program_id(0), pl.num_programs(0)
    x = [ref[...] for ref in pieces]
    x = x[0] if len(x) == 1 else jnp.concatenate(x, axis=0)
    for weight, total in zip(weights, totals):
        term = jnp.dot(x, weight[...], preferred_element_type=jnp.float32)

        @pl.when(step == 0)
        def _():
            total[...] = term

        @pl.when(step > 0)
        def _():
            total[...] = total[...] + term

    @pl.when(step == steps - 1)
    def _():
        height = sum(heights[0])
        for i, out in enumerate(outs):
            rows = slice(i * height, (i + 1) * height)
            start = 0
            for h in range(kv_heads):
                for total in totals:
                    width = total.shape[1] // kv_heads
                    part = total[rows, h * width : (h + 1) * width]
                    out[:, start : start + width] = part.astype(out.dtype)
                    start += width


def project(slots, weights, kv_heads=1):
    heights = [[x.shape[0] for x in slot] for slot in slots]
    depth = slots[0][0].shape[1]
    block = depth // 8
    widths = [w.shape[1] for w in weights]
    shape = jax.ShapeDtypeStruct((sum(heights[0]), sum(widths)), jnp.bfloat16)
    rows = sum(map(sum, heights))
    return list(
        pl.pallas_call(
            functools.partial(project_kernel, heights, len(weights), kv_heads),
            grid=(depth // block,),
            in_specs=[pl.BlockSpec((h, block), lambda k: (0, k)) for hs in heights for h in hs]
            + [pl.BlockSpec((block, width), lambda k: (k, 0)) for width in widths],
            out_specs=[pl.BlockSpec(shape.shape, lambda k: (0, 0))] * len(slots),
            out_shape=[shape] * len(slots),
            scratch_shapes=[pltpu.VMEM((rows, w), jnp.float32) for w in widths],
            compiler_params=pltpu.CompilerParams(vmem_limit_bytes=VMEM_LIMIT),
            cost_estimate=SMALL,
            name="project",
        )(*sum(map(list, slots), []), *weights)
    )


def per_device(tokens, memory_embed, norm_gain, w_query, w_key, value_weight, w_out, retain):
    planes = Planes(lax.axis_size("tensor"))
    turns = list(planes.turns)
    me = lax.axis_index("tensor")
    seg, seg_count = lax.axis_index("seg"), lax.axis_size("seg")
    core, chip, chips = seg % 2, seg // 2, seg_count // 2
    is_end = (me < planes.quarter) | (me >= 3 * planes.quarter)
    worker = jnp.where(is_end, planes.partner(me), me)
    heads, kv_heads = w_query.shape[1] // HEAD, w_key.shape[1] // HEAD
    groups = heads // kv_heads
    lay = Layout(planes.count, tokens.shape[0], memory_embed.shape[0], groups)
    back, lend = planes.give_back(), planes.lend()

    depth = w_query.shape[0] // seg_count

    lent_shares = []
    for h in range(kv_heads):
        cuts = []
        for array, wide in ((w_query, lay.wide), (w_key, HEAD), (value_weight, HEAD)):
            cuts.append(lax.dynamic_slice(array, (seg * depth, h * wide), (depth, wide)))
        lent_shares.append(jnp.concatenate(cuts, axis=1))
    half = w_out.shape[1] // 2
    width = half // chips
    share = lax.dynamic_slice_in_dim(w_out, core * half + chip * width, width, 1)

    places = [me, planes.partner(me)]
    for turn in turns:
        peer = planes.peer(worker, turn)
        places += [peer, planes.partner(peer)]
    places = jnp.stack(places).astype(jnp.int32)
    ids = (core * chips + ring_order()).astype(jnp.int32)
    own_weights = [w_query, w_key, value_weight]
    numbers = [0, 1] + [2 + 2 * at for at in range(len(turns))]
    far_numbers = [3 + 2 * at for at in range(len(turns))]
    half_rows = lay.height // 2
    own, taken = {}, [{} for _ in range(kv_heads)]

    lent = [hop(lent_shares[0], lend)]
    peers = [hop(share, planes.exchange(turn)) for turn in turns]
    near_back = hop(share, back)
    rates = jnp.concatenate([retain, hop(retain, lend)], axis=1)
    gain = tie(norm_gain, share, lent_shares)
    rows = jnp.concatenate(
        [pad_rows(rms_rows(tokens, gain)), pad_rows(rms_rows(memory_embed, gain))], axis=0
    )
    lent, peers, near_back, rows, share, lent_shares, rates, places, ids = gate(
        lent, peers, near_back, rows, share, lent_shares, rates, places, ids
    )

    lent_all = [lax.all_gather(lent[0], "seg", axis=0, tiled=True)]
    rows_a = [hop(rows[:half_rows], lend)]
    near_rows = [hop(rows, planes.exchange(turn)) for turn in turns]
    rings = [ChipRing(jnp.where(is_end, near_back, peers[0]))]
    (own[0],) = project([[rows]], own_weights, kv_heads)
    rates = seg_double(rates, 1)
    lent += [hop(tie(part, own[0]), lend) for part in lent_shares[1:]]
    held = (rings[0].right, rings[0].left)
    rows_a, near_rows, held, own, rows, share, peers, rates, lent = gate(
        rows_a, near_rows, held, own, rows, share, peers, rates, lent
    )
    rings[0].right, rings[0].left = held

    lent_all += [lax.all_gather(part, "seg", axis=0, tiled=True) for part in lent[1:]]
    far_rows = [[hop(rows_a[0], planes.exchange(turn))] for turn in turns]
    rows_a.append(hop(rows[half_rows:], lend))
    ends = [hop(piece, back) for piece in peers]
    rings[0].close()
    rates = seg_double(rates, 2)
    known = [[rows], rows_a] + [[x] for x in near_rows]
    own.update(zip(numbers[2:], project(known[2:], own_weights, kv_heads)))
    first = tie(lent_all[0], own[2])
    here = [known[0]] + known[2:]
    taken[0].update(zip([0] + numbers[2:], project(here, [first])))
    far_rows, ends, rings[0].last, own, known, first, share, rates, taken = gate(
        far_rows, ends, rings[0].last, own, known, first, share, rates, taken
    )
    lent_all[0] = first
    bit = 4
    while bit < seg_count:
        rates = seg_double(rates, bit)
        bit *= 2

    for parts, turn in zip(far_rows, turns):
        parts.append(hop(known[1][1], planes.exchange(turn)))
    near = hop(share, lend)
    (own[1],) = project([known[1]], own_weights, kv_heads)
    (taken[0][1],) = project([known[1]], [tie(first, own[1])])
    for h in range(1, kv_heads):
        lent_all[h] = tie(lent_all[h], taken[h - 1])
        taken[h].update(zip(numbers, project(known, [lent_all[h]])))
    far_rows, near, taken, own, ends, rates = gate(far_rows, near, taken, own, ends, rates)

    cut = near.shape[0] // 2
    cuts = (near[:cut], near[cut:])
    far_near = [[hop(part, planes.exchange(turn)) for part in cuts] for turn in turns]
    for end, mid in zip(ends, peers[1:] + [near]):
        rings.append(ChipRing(jnp.where(is_end, end, mid)))
    own.update(zip(far_numbers, project(far_rows, own_weights, kv_heads)))
    order = range(planes.count)
    own_slots = [own[slot] for slot in order]
    own_units = [Unit(lay, places, own_slots, h) for h in range(kv_heads)]
    writes = jnp.concatenate([u.memory_write() for u in own_units], axis=0)

    def first_lent(dep):
        taken[0].update(zip(far_numbers, project([tie(x, dep) for x in far_rows], [lent_all[0]])))
        return taken[0][far_numbers[-1]]

    backs = []

    def close_rings():
        held = gate(*[(ring.right, ring.left) for ring in rings[1:]])
        for ring, (right, left) in zip(rings[1:], held):
            ring.right, ring.left = right, left
        halves = gate(*[ring.halves() for ring in rings[1:]])
        for ring, pair in zip(rings[1:], halves):
            ring.close(pair)
        return halves

    def far_lent(dep, h):
        part, dep, early = gate(lent_all[h], dep, [parts[0] for parts in far_near])
        if h == 1:
            backs.extend([hop(piece, back)] for piece in early)
        xs = [[tie(x, dep) for x in xs] for xs in far_rows]
        taken[h].update(zip(far_numbers, project(xs, [part])))
        return taken[h][far_numbers[-1]]

    lent_writes = []

    def write_lent(dep):
        dep = tie(dep, close_rings())
        lent_units.extend(Unit(lay, places, [part[slot] for slot in order]) for part in taken)
        lent_writes.extend(unit.tied(dep).memory_write() for unit in lent_units)
        return lent_writes[-1]

    lent_units = []
    works = [first_lent]
    works += [functools.partial(far_lent, h=h) for h in range(1, kv_heads)]
    works.append(write_lent)
    state, _ = relay(writes, rates[:, :heads], works)

    far_near, own_slots, writes, state, backs = gate(
        far_near, own_slots, lent_writes, state, backs
    )
    if kv_heads == 1:
        backs = [[hop(parts[0], back)] for parts in far_near]
    for parts, returned in zip(far_near, backs):
        returned.append(hop(parts[1], back))
    own_units = [Unit(lay, places, own_slots, h) for h in range(kv_heads)]
    writes = jnp.concatenate(writes, axis=0)

    def cross(arrays):
        return (
            arrays[0],
            hop(arrays[1], back),
            [hop(arrays[2 + 2 * at], planes.exchange(turn)) for at, turn in enumerate(turns)],
            [hop(arrays[3 + 2 * at], planes.far_back(turn)) for at, turn in enumerate(turns)],
        )

    parts = 2 if groups % 2 == 0 else 1
    mixed_own, crossed = [[] for _ in range(kv_heads)], []

    def attend_own(dep, h, part):
        unit, some = own_units[h].tied(dep), groups // parts
        if h == 0 and part == parts - 1:
            unit = unit.tied(rings[-1].last)
        mixed_own[h] = unit.attend(
            state[h * groups : (h + 1) * groups], part * some, some, part, parts, mixed_own[h]
        )
        if h < kv_heads - 1 and part == parts - 1:
            crossed.append(cross(mixed_own[h]))
        return mixed_own[h][0]

    works = [
        functools.partial(attend_own, h=h, part=part)
        for h in range(kv_heads)
        for part in range(parts)
    ]

    def attend_rest(dep):
        for number, work in enumerate(works[2:]):
            dep = work(dep if number == 0 else tie(dep, [c[2:] for c in crossed]))
        return dep

    passed = works[:2] + [attend_rest] * (len(works) > 2)
    lent_state, _ = relay(writes, rates[:, heads:], passed)
    last = rings[-1].last
    lent_state, last_own, backs, last = gate(lent_state, mixed_own[-1], backs, last)
    rings[-1].last = last

    late = len(rings)
    for parts, returned in zip(far_near, backs):
        stage = [jnp.where(is_end, e, m) for e, m in zip(returned, parts)]
        rings.append(ChipRing(tie(jnp.concatenate(stage, axis=0), last)))

    crossed.append(cross(last_own))
    for h, unit in enumerate(lent_units):
        if h == len(lent_units) - 1:
            unit = unit.tied(crossed[kv_heads - 1][1:])
        crossed.append(cross(unit.attend(lent_state[h * groups : (h + 1) * groups])))

    def join(arrays):
        both = jnp.concatenate(arrays, axis=1)
        return both[:, : heads * HEAD], both[:, heads * HEAD :]

    home = join([c[0] for c in crossed])
    returned = join([c[1] for c in crossed])
    near_mixed = [join([c[2][at] for c in crossed]) for at in range(len(turns))]
    far_mixed = [join([c[3][at] for c in crossed]) for at in range(len(turns))]
    ends = [returned[1], returned[0]] + [m[0] for m in far_mixed] + [m[1] for m in far_mixed]
    mids = [home[0]] + [m[0] for m in near_mixed] + [home[1]] + [m[1] for m in near_mixed]
    mixed = jnp.concatenate([jnp.where(is_end, e, m) for e, m in zip(ends, mids)], axis=1)

    held = [(ring.right, ring.left) for ring in rings[late:]]
    mixed, held = gate(mixed, held)
    for ring, (right, left) in zip(rings[late:], held):
        ring.right, ring.left = right, left
        ring.close()
    other = swap_cores(mixed)
    base = pad_rows(tokens)
    begun = output_product(mixed, other, base, w_out, ids, [r.pieces() for r in rings[:late]])
    for ring in rings[late:]:
        ring.last = tie(ring.last, begun)
    far_pieces = [ring.pieces() for ring in rings[late:]]
    result, other = output_product(mixed, other, base, w_out, ids, far_pieces, begun)
    other = swap_cores(other)
    start = (1 - core) * half
    base = lax.dynamic_slice_in_dim(base, start, half, 1)
    other = (base.astype(jnp.float32) + other.astype(jnp.float32)).astype(jnp.bfloat16)
    result = lax.dynamic_update_slice_in_dim(result, other, start, 1)
    return result[: tokens.shape[0]]


def solution(mesh):
    return jax.shard_map(
        per_device,
        mesh=mesh,
        in_specs=(
            P(("seg", "tensor"), None),
            P("tensor", None),
            P(),
            P(None, "tensor"),
            P(None, "tensor"),
            P(None, "tensor"),
            P("tensor", None),
            P("seg", "tensor"),
        ),
        out_specs=P(("seg", "tensor"), None),
        check_vma=False,
    )
```

```python
import functools

import jax
import jax.numpy as jnp
from jax import lax
from jax.experimental import pallas as pl
from jax.experimental.pallas import tpu as pltpu
from jax.sharding import PartitionSpec as P

HEAD = 128
EPSILON = 1e-05
SCALE = HEAD ** (-0.5)
LOG2E = 1.4426950408889634
STATE_ROWS = HEAD + 16
VMEM_LIMIT = 48 * 1024 * 1024
SMALL = pl.CostEstimate(flops=1, bytes_accessed=1, transcendentals=0)


def rms_rows(rows, norm_gain):
    widened = rows.astype(jnp.float32)
    scale_rows = lax.rsqrt(jnp.mean(widened * widened, axis=-1, keepdims=True) + EPSILON)
    return (widened * scale_rows * norm_gain.astype(jnp.float32)).astype(jnp.bfloat16)


def feature_map(inputs):
    return jnp.exp(jnp.minimum(inputs, 0.0)) + jnp.maximum(inputs, 0.0)


def tie(value, *others):
    return lax.optimization_barrier((value,) + others)[0]


def gate(*values):
    return lax.optimization_barrier(values)


class Planes:
    def __init__(self, count):
        self.count = count
        self.quarter = count // 4
        self.workers = range(self.quarter, 3 * self.quarter)
        self.ends = [i for i in range(count) if i not in self.workers]
        self.turns = range(1, count // 2)

    def partner(self, index):
        return index ^ self.quarter

    def peer(self, index, turn):
        return self.quarter + ((index - self.quarter) ^ turn)

    def lend(self):
        return [(e, self.partner(e)) for e in self.ends]

    def give_back(self):
        return [(w, self.partner(w)) for w in self.workers]

    def pairs(self):
        return [(i, self.partner(i)) for i in range(self.count)]

    def exchange(self, turn):
        return [(w, self.peer(w, turn)) for w in self.workers]

    def far_back(self, turn):
        return [(w, self.partner(self.peer(w, turn))) for w in self.workers]


def hop(block, pairs):
    return lax.ppermute(block, "tensor", pairs)


def seg_cycle(chips):
    half = chips // 2
    return list(range(half)) + list(range(chips - 1, half - 1, -1))


def swap_cores(block):
    return lax.ppermute(block, "seg", [(i, i ^ 1) for i in range(lax.axis_size("seg"))])


def ring_order():
    chips = lax.axis_size("seg") // 2
    cycle = seg_cycle(chips)
    place_of = [cycle.index(c) for c in range(chips)]
    place = jnp.array(place_of, jnp.int32)[lax.axis_index("seg") // 2]
    steps = [0] + [s for turn in range(1, chips // 2) for s in (-turn, turn)] + [chips // 2]
    return jnp.array(cycle, jnp.int32)[(place + jnp.array(steps) + chips) % chips]


class ChipRing:
    def __init__(self, block, straight=False):
        self.chips = lax.axis_size("seg") // 2
        self.cycle = seg_cycle(self.chips)
        self.block, self.right, self.left, self.last = block, [block], [block], None
        for _ in range(1, self.chips // 2):
            self.right.append(self.step(self.right[-1], 1))
            self.left.append(self.step(self.left[-1], -1))
        if straight:
            self.last = (self.step(block, self.chips // 2),)

    def step(self, part, distance):
        route = [
            (self.cycle[i] * 2 + c, self.cycle[(i + distance) % self.chips] * 2 + c)
            for i in range(self.chips)
            for c in range(2)
        ]
        return lax.ppermute(part, "seg", route)

    def halves(self):
        half = self.block.shape[0] // 2
        return self.right[-1][:half], self.left[-1][half:]

    def close(self, halves=None):
        right, left = halves or self.halves()
        self.last = (self.step(right, 1), self.step(left, -1))

    def pieces(self):
        found = [(self.block,)]
        for turn in range(1, self.chips // 2):
            found += [(self.right[turn],), (self.left[turn],)]
        return found + [self.last]


def seg_double(values, bit):
    size = lax.axis_size("seg")
    got = lax.ppermute(values, "seg", [(i, i ^ bit) for i in range(size)])
    upper = (lax.axis_index("seg") // bit) % 2 == 1
    return jnp.concatenate(
        [jnp.where(upper, got, values), jnp.where(upper, values, got)], axis=0
    )


def pad_to(value, unit):
    return -(-value // unit) * unit


def pad_rows(array, unit=16):
    return jnp.pad(array, ((0, pad_to(array.shape[0], unit) - array.shape[0]), (0, 0)))


def nt_dot(a, b):
    return lax.dot_general(a, b, (((1,), (1,)), ((), ())), preferred_element_type=jnp.float32)


class Layout:
    def __init__(self, slots, rows, mem, groups):
        self.slots, self.rows, self.mem, self.groups = slots, rows, mem, groups
        self.stride, self.mem_stride = pad_to(rows, 16), pad_to(mem, 16)
        self.height = self.stride + self.mem_stride
        self.spread = slots * self.stride
        self.mem_spread = slots * self.mem_stride
        self.full = pad_to(self.spread, 128)
        self.wide = groups * HEAD
        self.unit = (groups + 2) * HEAD

    def valid(self, ids):
        return lax.rem(ids, self.stride) < self.rows

    def mem_valid(self, ids):
        return lax.rem(ids, self.mem_stride) < self.mem


def memory_kernel(lay, place_ref, *refs):
    slots, out_ref, key_all, value_all, mem_all = refs[: lay.slots], *refs[lay.slots :]
    wide = lay.wide
    for i, ref in enumerate(slots):
        start = pl.multiple_of(place_ref[i] * lay.stride, 16)
        key_all[pl.ds(start, lay.stride), :] = ref[: lay.stride, wide : wide + HEAD]
        value_all[pl.ds(start, lay.stride), :] = ref[: lay.stride, wide + HEAD :]
        start = pl.multiple_of(place_ref[i] * lay.mem_stride, 16)
        mem_all[pl.ds(start, lay.mem_stride), :] = ref[lay.stride :, :]
    k_tok, v_tok = key_all[...], value_all[...]
    k_mem, v_mem = mem_all[:, wide : wide + HEAD], mem_all[:, wide + HEAD :]
    mem = lay.mem_spread
    row_ids = lax.broadcasted_iota(jnp.int32, (mem, mem), 0)
    col_ids = lax.broadcasted_iota(jnp.int32, (mem, mem), 1)
    keep = row_ids >= col_ids
    feat = feature_map(k_mem.astype(jnp.float32))
    if lay.mem_stride != lay.mem:
        keep = keep & lay.mem_valid(col_ids)
        feat_ids = lax.broadcasted_iota(jnp.int32, (mem, HEAD), 0)
        feat = jnp.where(lay.mem_valid(feat_ids), feat, 0.0)
    feat_sum = jnp.sum(feat, axis=0, keepdims=True)
    feat_cast = feat.astype(jnp.bfloat16)
    for g in range(lay.groups):
        q = mem_all[:, g * HEAD : (g + 1) * HEAD]
        s_tok = nt_dot(q, k_tok)
        if lay.stride != lay.rows:
            ids = lax.broadcasted_iota(jnp.int32, (mem, lay.spread), 1)
            s_tok = jnp.where(lay.valid(ids), s_tok, -1e30)
        s_mem = jnp.where(keep, nt_dot(q, k_mem), -1e30)
        top = jnp.maximum(
            jnp.max(s_tok, axis=1, keepdims=True), jnp.max(s_mem, axis=1, keepdims=True)
        )
        p_tok = jnp.exp2((s_tok - top) * (SCALE * LOG2E))
        p_mem = jnp.exp2((s_mem - top) * (SCALE * LOG2E))
        total = jnp.sum(p_tok, axis=1, keepdims=True) + jnp.sum(p_mem, axis=1, keepdims=True)
        soft = jnp.dot(
            p_tok.astype(jnp.bfloat16), v_tok, preferred_element_type=jnp.float32
        ) + jnp.dot(p_mem.astype(jnp.bfloat16), v_mem, preferred_element_type=jnp.float32)
        soft = soft / total
        out_ref[g, :HEAD, :] = lax.dot_general(
            feat_cast,
            soft.astype(jnp.bfloat16),
            (((0,), (0,)), ((), ())),
            preferred_element_type=jnp.float32,
        )
        out_ref[g, HEAD:, :] = jnp.broadcast_to(feat_sum, (STATE_ROWS - HEAD, HEAD))


def read_state(query, state, sums):
    feat = feature_map(query.astype(jnp.float32)).astype(jnp.bfloat16)
    numerator = jnp.dot(feat, state.astype(jnp.bfloat16), preferred_element_type=jnp.float32)
    sums = jnp.broadcast_to(sums, (HEAD, HEAD)).astype(jnp.bfloat16)
    return numerator / (nt_dot(feat, sums) + 1.0)


def token_kernel(lay, first_head, heads, begun, place_ref, *refs):
    count, stride, wide = lay.slots, lay.stride, lay.wide
    slots, refs = refs[:count], refs[count:]
    state_ref, refs = refs[0], refs[1 + begun :]
    outs, (query_all, key_all, value_all, out_all) = refs[:count], refs[count:]
    if lay.full > lay.spread:
        tail = (lay.full - lay.spread, HEAD)
        key_all[lay.spread :, :] = jnp.zeros(tail, key_all.dtype)
        value_all[lay.spread :, :] = jnp.zeros(tail, value_all.dtype)
    for i, ref in enumerate(slots):
        rows = pl.ds(pl.multiple_of(place_ref[i] * stride, 16), stride)
        query_all[rows, :] = ref[:stride, first_head * HEAD : (first_head + heads) * HEAD]
        key_all[rows, :] = ref[:stride, wide : wide + HEAD]
        value_all[rows, :] = ref[:stride, wide + HEAD :]

    for block in range(count):
        first = block * stride
        low = first // 128 * 128
        high = min(pad_to(first + stride, 128), lay.full)
        k_diag, v_diag = key_all[low:high, :], value_all[low:high, :]
        row_ids = lax.broadcasted_iota(jnp.int32, (stride, high - low), 0) + first
        col_ids = lax.broadcasted_iota(jnp.int32, (stride, high - low), 1) + low
        keep = row_ids >= col_ids
        if stride != lay.rows:
            keep = keep & lay.valid(col_ids)

        def one_head(g, carry, first=first, low=low, k_diag=k_diag, v_diag=v_diag, keep=keep):
            lanes = pl.ds(pl.multiple_of(g * HEAD, HEAD), HEAD)
            q = query_all[first : first + stride, lanes]
            at = first_head + g
            s_diag = jnp.where(keep, nt_dot(q, k_diag), -1e30)
            top = jnp.max(s_diag, axis=1, keepdims=True)
            if low > 0:
                s_prev = nt_dot(q, key_all[:low, :])
                if stride != lay.rows:
                    ids = lax.broadcasted_iota(jnp.int32, (stride, low), 1)
                    s_prev = jnp.where(lay.valid(ids), s_prev, -1e30)
                top = jnp.maximum(top, jnp.max(s_prev, axis=1, keepdims=True))
            p_diag = jnp.exp2((s_diag - top) * (SCALE * LOG2E))
            total = jnp.sum(p_diag, axis=1, keepdims=True)
            soft = jnp.dot(
                p_diag.astype(jnp.bfloat16), v_diag, preferred_element_type=jnp.float32
            )
            if low > 0:
                p_prev = jnp.exp2((s_prev - top) * (SCALE * LOG2E))
                total = total + jnp.sum(p_prev, axis=1, keepdims=True)
                soft = soft + jnp.dot(
                    p_prev.astype(jnp.bfloat16),
                    value_all[:low, :],
                    preferred_element_type=jnp.float32,
                )
            state, sums = state_ref[at, :HEAD, :], state_ref[at, HEAD : HEAD + 1, :]
            out_all[first : first + stride, lanes] = soft / total + read_state(q, state, sums)
            return carry

        lax.fori_loop(0, heads, one_head, 0)

    for i, ref in enumerate(outs):
        rows = pl.ds(pl.multiple_of(place_ref[i] * stride, 16), stride)
        ref[...] = out_all[rows, :].astype(ref.dtype)


class Unit:
    def __init__(self, lay, places, slots, at=0):
        self.lay, self.places, self.slots, self.at = lay, places, slots, at

    def tied(self, *others):
        return Unit(self.lay, self.places, [tie(s, *others) for s in self.slots], self.at)

    def slot_specs(self):
        lay, at = self.lay, self.at
        return [pl.BlockSpec((lay.height, lay.unit), lambda i, *_: (0, at))] * lay.slots

    def state_spec(self):
        return pl.BlockSpec((self.lay.groups, STATE_ROWS, HEAD), lambda i, *_: (0, 0, 0))

    def memory_write(self):
        lay = self.lay
        return pl.pallas_call(
            functools.partial(memory_kernel, lay),
            grid_spec=pltpu.PrefetchScalarGridSpec(
                num_scalar_prefetch=1,
                grid=(1,),
                in_specs=self.slot_specs(),
                out_specs=self.state_spec(),
                scratch_shapes=[
                    pltpu.VMEM((lay.spread, HEAD), jnp.bfloat16),
                    pltpu.VMEM((lay.spread, HEAD), jnp.bfloat16),
                    pltpu.VMEM((lay.mem_spread, lay.unit), jnp.bfloat16),
                ],
            ),
            out_shape=jax.ShapeDtypeStruct((lay.groups, STATE_ROWS, HEAD), jnp.float32),
            compiler_params=pltpu.CompilerParams(vmem_limit_bytes=VMEM_LIMIT),
            cost_estimate=SMALL,
            name="memory_write",
        )(self.places, *self.slots)

    def attend(self, state, first_head=0, heads=None, block=0, blocks=1, begun=()):
        lay = self.lay
        heads = heads or lay.groups
        wide = heads * HEAD
        out_spec = pl.BlockSpec((lay.stride, wide), lambda i, *_: (0, block))
        return list(
            pl.pallas_call(
                functools.partial(token_kernel, lay, first_head, heads, len(begun)),
                grid_spec=pltpu.PrefetchScalarGridSpec(
                    num_scalar_prefetch=1,
                    grid=(1,),
                    in_specs=self.slot_specs()
                    + [self.state_spec()]
                    + [pl.BlockSpec(memory_space=pl.ANY)] * len(begun),
                    out_specs=[out_spec] * lay.slots,
                    scratch_shapes=[
                        pltpu.VMEM((lay.spread, wide), jnp.bfloat16),
                        pltpu.VMEM((lay.full, HEAD), jnp.bfloat16),
                        pltpu.VMEM((lay.full, HEAD), jnp.bfloat16),
                        pltpu.VMEM((lay.spread, wide), jnp.float32),
                    ],
                ),
                out_shape=[jax.ShapeDtypeStruct((lay.stride, blocks * wide), jnp.bfloat16)]
                * lay.slots,
                input_output_aliases={2 + lay.slots + i: i for i in range(len(begun))},
                compiler_params=pltpu.CompilerParams(vmem_limit_bytes=VMEM_LIMIT),
                cost_estimate=SMALL,
                name="token_attention",
            )(self.places, *self.slots, state, *begun)
        )


def relay(writes, rates, works):
    size = lax.axis_size("seg")
    me = lax.axis_index("seg")
    ids = lax.broadcasted_iota(jnp.int32, (size, 1), 0)

    def product(mask):
        return jnp.prod(jnp.where(mask, rates, 1.0), axis=0)[:, None, None]

    total = writes
    prefix = jnp.zeros_like(writes)
    results = []
    bit = 1
    while bit < size:
        route = [(i, i ^ bit) for i in range(size)]
        sent = total.astype(jnp.bfloat16)
        got = lax.ppermute(sent, "seg", route)
        if len(results) < len(works):
            results.append(works[len(results)](sent))
            got = tie(got, results[-1])
        got = got.astype(jnp.float32)
        mine = ids // bit == me // bit
        theirs = ids // bit == (me // bit) ^ 1
        upper = (me // bit) % 2 == 1
        prefix = jnp.where(upper, product(mine & (ids < me)) * got + prefix, prefix)
        total = jnp.where(upper, product(mine) * got + total, product(theirs) * total + got)
        bit *= 2
    for work in works[len(results) :]:
        results.append(work(prefix))
    return prefix, results


def output_kernel(plan, final, ids_ref, mixed_ref, other_ref, own_ref, *refs):
    count = 1 + max(p for row in plan for p in row if p is not None)
    piece_refs, refs = refs[:count], refs[count:]
    if final:
        base_ref, begun_ref, out_ref, far_ref, both, weights, sems = refs
    else:
        out_ref, both, weights, sems = refs
    rows = mixed_ref.shape[0]
    blocks = len(plan)
    width = weights.shape[2]
    step = pl.program_id(0)

    def start(at):
        slot = lax.rem(at, 2)
        for b in range(blocks):

            @pl.when(at == b)
            def _():
                row = 0
                for index in plan[b]:
                    if index is None:
                        columns = pl.ds(pl.multiple_of(ids_ref[b] * width, 128), width)
                        part = own_ref.at[:, columns]
                    else:
                        part = piece_refs[index]
                    high = part.shape[0]
                    pltpu.make_async_copy(
                        part, weights.at[slot, pl.ds(row, high), :], sems.at[slot]
                    ).start()
                    row += high

    @pl.when(step == 0)
    def _():
        start(jnp.int32(0))
        both[:rows, :] = mixed_ref[...]
        both[rows:, :] = other_ref[...]

    @pl.when(step + 1 < blocks)
    def _():
        start(step + 1)

    slot = lax.rem(step, 2)
    pltpu.make_async_copy(weights.at[slot], weights.at[slot], sems.at[slot]).wait()
    term = jnp.dot(both[...], weights[slot], preferred_element_type=jnp.float32)
    if final:
        term = term + begun_ref[0].astype(jnp.float32)
        base = base_ref[...].astype(jnp.float32)
        out_ref[...] = (base + term[:rows, :]).astype(out_ref.dtype)
        far_ref[...] = term[rows:, :].astype(far_ref.dtype)
    else:
        out_ref[0] = term.astype(out_ref.dtype)


def output_product(mixed, other, tokens, w_out, ids, gathered, begun=None):
    rows = mixed.shape[0]
    final = begun is not None
    blocks = len(gathered[0])
    width = w_out.shape[1] // (2 * blocks)
    plan, pieces = [], []
    for b in range(blocks):
        row = [] if final else [None]
        for parts in gathered:
            row += range(len(pieces), len(pieces) + len(parts[b]))
            pieces += parts[b]
        plan.append(row)
    depth = w_out.shape[0] * (len(gathered) + (0 if final else 1))
    whole = pl.BlockSpec((rows, width), lambda c, ids: (0, ids[c]))
    half = pl.BlockSpec((rows, width), lambda c, ids: (0, lax.rem(ids[c], blocks)))
    sums = pl.BlockSpec((1, 2 * rows, width), lambda c, ids: (c, 0, 0))
    mixed_spec = pl.BlockSpec(mixed.shape, lambda c, ids: (0, 0))
    if final:
        shapes = [
            jax.ShapeDtypeStruct((rows, w_out.shape[1]), jnp.bfloat16),
            jax.ShapeDtypeStruct((rows, w_out.shape[1] // 2), jnp.bfloat16),
        ]
    else:
        shapes = jax.ShapeDtypeStruct((blocks, 2 * rows, width), jnp.bfloat16)
    return pl.pallas_call(
        functools.partial(output_kernel, plan, final),
        grid_spec=pltpu.PrefetchScalarGridSpec(
            num_scalar_prefetch=1,
            grid=(blocks,),
            in_specs=[mixed_spec] * 2
            + [pl.BlockSpec(memory_space=pl.ANY)] * (1 + len(pieces))
            + ([whole, sums] if final else []),
            out_specs=[whole, half] if final else sums,
            scratch_shapes=[
                pltpu.VMEM((2 * rows, depth), jnp.bfloat16),
                pltpu.VMEM((2, depth, width), jnp.bfloat16),
                pltpu.SemaphoreType.DMA((2,)),
            ],
        ),
        out_shape=shapes,
        compiler_params=pltpu.CompilerParams(vmem_limit_bytes=VMEM_LIMIT),
        cost_estimate=SMALL,
        name="output_product",
    )(ids, mixed, other, w_out, *pieces, *((tokens, begun) if final else ()))


def project_kernel(heights, parts, kv_heads, *refs):
    pieces = [ref for ref in refs[: sum(map(len, heights))]]
    refs = refs[len(pieces) :]
    weights, outs = refs[:parts], refs[parts : parts + len(heights)]
    totals = refs[parts + len(heights) :]
    step, steps = pl.program_id(0), pl.num_programs(0)
    x = [ref[...] for ref in pieces]
    x = x[0] if len(x) == 1 else jnp.concatenate(x, axis=0)
    for weight, total in zip(weights, totals):
        term = jnp.dot(x, weight[...], preferred_element_type=jnp.float32)

        @pl.when(step == 0)
        def _():
            total[...] = term

        @pl.when(step > 0)
        def _():
            total[...] = total[...] + term

    @pl.when(step == steps - 1)
    def _():
        height = sum(heights[0])
        for i, out in enumerate(outs):
            rows = slice(i * height, (i + 1) * height)
            start = 0
            for h in range(kv_heads):
                for total in totals:
                    width = total.shape[1] // kv_heads
                    part = total[rows, h * width : (h + 1) * width]
                    out[:, start : start + width] = part.astype(out.dtype)
                    start += width


def project(slots, weights, kv_heads=1):
    heights = [[x.shape[0] for x in slot] for slot in slots]
    depth = slots[0][0].shape[1]
    block = depth // 8
    widths = [w.shape[1] for w in weights]
    shape = jax.ShapeDtypeStruct((sum(heights[0]), sum(widths)), jnp.bfloat16)
    rows = sum(map(sum, heights))
    return list(
        pl.pallas_call(
            functools.partial(project_kernel, heights, len(weights), kv_heads),
            grid=(depth // block,),
            in_specs=[pl.BlockSpec((h, block), lambda k: (0, k)) for hs in heights for h in hs]
            + [pl.BlockSpec((block, width), lambda k: (k, 0)) for width in widths],
            out_specs=[pl.BlockSpec(shape.shape, lambda k: (0, 0))] * len(slots),
            out_shape=[shape] * len(slots),
            scratch_shapes=[pltpu.VMEM((rows, w), jnp.float32) for w in widths],
            compiler_params=pltpu.CompilerParams(vmem_limit_bytes=VMEM_LIMIT),
            cost_estimate=SMALL,
            name="project",
        )(*sum(map(list, slots), []), *weights)
    )


def per_device(tokens, memory_embed, norm_gain, w_query, w_key, value_weight, w_out, retain):
    planes = Planes(lax.axis_size("tensor"))
    turns = list(planes.turns)
    me = lax.axis_index("tensor")
    seg, seg_count = lax.axis_index("seg"), lax.axis_size("seg")
    core, chip, chips = seg % 2, seg // 2, seg_count // 2
    is_end = (me < planes.quarter) | (me >= 3 * planes.quarter)
    worker = jnp.where(is_end, planes.partner(me), me)
    heads, kv_heads = w_query.shape[1] // HEAD, w_key.shape[1] // HEAD
    groups = heads // kv_heads
    lay = Layout(planes.count, tokens.shape[0], memory_embed.shape[0], groups)
    back, lend = planes.give_back(), planes.lend()

    depth = w_query.shape[0] // seg_count

    lent_shares = []
    for h in range(kv_heads):
        cuts = []
        for array, wide in ((w_query, lay.wide), (w_key, HEAD), (value_weight, HEAD)):
            cuts.append(lax.dynamic_slice(array, (seg * depth, h * wide), (depth, wide)))
        lent_shares.append(jnp.concatenate(cuts, axis=1))
    half = w_out.shape[1] // 2
    width = half // chips
    share = lax.dynamic_slice_in_dim(w_out, core * half + chip * width, width, 1)

    places = [me, planes.partner(me)]
    for turn in turns:
        peer = planes.peer(worker, turn)
        places += [peer, planes.partner(peer)]
    places = jnp.stack(places).astype(jnp.int32)
    ids = (core * chips + ring_order()).astype(jnp.int32)
    own_weights = [w_query, w_key, value_weight]
    numbers = [0, 1] + [2 + 2 * at for at in range(len(turns))]
    far_numbers = [3 + 2 * at for at in range(len(turns))]
    half_rows = lay.height // 2
    own, taken = {}, [{} for _ in range(kv_heads)]

    lent = [hop(lent_shares[0], lend)]
    peers = [hop(share, planes.exchange(turn)) for turn in turns]
    near_back = hop(share, back)
    rates = jnp.concatenate([retain, hop(retain, lend)], axis=1)
    gain = tie(norm_gain, share, lent_shares)
    rows = jnp.concatenate(
        [pad_rows(rms_rows(tokens, gain)), pad_rows(rms_rows(memory_embed, gain))], axis=0
    )
    cut = share.shape[0] // 2
    shares = [share[:cut], share[cut:]]
    row_parts = [rows[:half_rows], rows[half_rows:]]
    lent, peers, near_back, rows, row_parts, shares, lent_shares, rates, places, ids = gate(
        lent, peers, near_back, rows, row_parts, shares, lent_shares, rates, places, ids
    )

    lent_all = [lax.all_gather(lent[0], "seg", axis=0, tiled=True)]
    rows_a = [hop(row_parts[0], lend)]
    near_rows = [hop(rows, planes.exchange(turn)) for turn in turns]
    rings = [ChipRing(jnp.where(is_end, near_back, peers[0]))]
    (own[0],) = project([[rows]], own_weights, kv_heads)
    rates = seg_double(rates, 1)
    lent += [hop(tie(part, own[0]), lend) for part in lent_shares[1:]]
    held = (rings[0].right, rings[0].left)
    rows_a, near_rows, held, own, rows, row_parts, shares, peers, rates, lent = gate(
        rows_a, near_rows, held, own, rows, row_parts, shares, peers, rates, lent
    )
    rings[0].right, rings[0].left = held

    lent_all += [lax.all_gather(part, "seg", axis=0, tiled=True) for part in lent[1:]]
    far_rows = [[hop(rows_a[0], planes.exchange(turn))] for turn in turns]
    rows_a.append(hop(row_parts[1], lend))
    ends = [hop(piece, back) for piece in peers]
    rings[0].close()
    rates = seg_double(rates, 2)
    known = [[rows], rows_a] + [[x] for x in near_rows]
    own.update(zip(numbers[2:], project(known[2:], own_weights, kv_heads)))
    first = tie(lent_all[0], own[2])
    here = [known[0]] + known[2:]
    taken[0].update(zip([0] + numbers[2:], project(here, [first])))
    far_rows, ends, rings[0].last, own, known, first, shares, rates, taken = gate(
        far_rows, ends, rings[0].last, own, known, first, shares, rates, taken
    )
    lent_all[0] = first
    bit = 4
    while bit < seg_count:
        rates = seg_double(rates, bit)
        bit *= 2

    for parts, turn in zip(far_rows, turns):
        parts.append(hop(known[1][1], planes.exchange(turn)))
    near = [hop(part, lend) for part in shares]
    (own[1],) = project([known[1]], own_weights, kv_heads)
    (taken[0][1],) = project([known[1]], [tie(first, own[1])])
    for h in range(1, kv_heads):
        lent_all[h] = tie(lent_all[h], taken[h - 1])
        taken[h].update(zip(numbers, project(known, [lent_all[h]])))
    far_rows, near, taken, own, ends, rates = gate(far_rows, near, taken, own, ends, rates)

    far_near = [[hop(part, planes.exchange(turn)) for part in near] for turn in turns]
    near = jnp.concatenate(near, axis=0)
    for end, mid in zip(ends, peers[1:] + [near]):
        rings.append(ChipRing(jnp.where(is_end, end, mid)))
    own.update(zip(far_numbers, project(far_rows, own_weights, kv_heads)))
    order = range(planes.count)
    own_slots = [own[slot] for slot in order]
    own_units = [Unit(lay, places, own_slots, h) for h in range(kv_heads)]
    writes = jnp.concatenate([u.memory_write() for u in own_units], axis=0)

    def first_lent(dep):
        taken[0].update(zip(far_numbers, project([tie(x, dep) for x in far_rows], [lent_all[0]])))
        return taken[0][far_numbers[-1]]

    backs = []

    def close_rings():
        held = gate(*[(ring.right, ring.left) for ring in rings[1:]])
        for ring, (right, left) in zip(rings[1:], held):
            ring.right, ring.left = right, left
        halves = gate(*[ring.halves() for ring in rings[1:]])
        for ring, pair in zip(rings[1:], halves):
            ring.close(pair)
        return halves

    def far_lent(dep, h):
        part, dep, early = gate(lent_all[h], dep, [parts[0] for parts in far_near])
        if h == 1:
            backs.extend([hop(piece, back)] for piece in early)
        xs = [[tie(x, dep) for x in xs] for xs in far_rows]
        taken[h].update(zip(far_numbers, project(xs, [part])))
        return taken[h][far_numbers[-1]]

    lent_writes = []

    def write_lent(dep):
        dep = tie(dep, close_rings())
        lent_units.extend(Unit(lay, places, [part[slot] for slot in order]) for part in taken)
        lent_writes.extend(unit.tied(dep).memory_write() for unit in lent_units)
        return lent_writes[-1]

    lent_units = []
    works = [first_lent]
    works += [functools.partial(far_lent, h=h) for h in range(1, kv_heads)]
    works.append(write_lent)
    state, _ = relay(writes, rates[:, :heads], works)

    far_near, own_slots, writes, state, backs = gate(
        far_near, own_slots, lent_writes, state, backs
    )
    if kv_heads == 1:
        backs = [[hop(parts[0], back)] for parts in far_near]
    for parts, returned in zip(far_near, backs):
        returned.append(hop(parts[1], back))
    own_units = [Unit(lay, places, own_slots, h) for h in range(kv_heads)]
    writes = jnp.concatenate(writes, axis=0)

    def cross(arrays):
        return (
            arrays[0],
            hop(arrays[1], back),
            [hop(arrays[2 + 2 * at], planes.exchange(turn)) for at, turn in enumerate(turns)],
            [hop(arrays[3 + 2 * at], planes.far_back(turn)) for at, turn in enumerate(turns)],
        )

    parts = 2 if groups % 2 == 0 else 1
    mixed_own, crossed = [[] for _ in range(kv_heads)], []

    def attend_own(dep, h, part):
        unit, some = own_units[h].tied(dep), groups // parts
        if h == 0 and part == parts - 1:
            unit = unit.tied(rings[-1].last)
        mixed_own[h] = unit.attend(
            state[h * groups : (h + 1) * groups], part * some, some, part, parts, mixed_own[h]
        )
        if h < kv_heads - 1 and part == parts - 1:
            crossed.append(cross(mixed_own[h]))
        return mixed_own[h][0]

    works = [
        functools.partial(attend_own, h=h, part=part)
        for h in range(kv_heads)
        for part in range(parts)
    ]

    def attend_rest(dep):
        for number, work in enumerate(works[2:]):
            dep = work(dep if number == 0 else tie(dep, [c[2:] for c in crossed]))
        return dep

    passed = works[:2] + [attend_rest] * (len(works) > 2)
    lent_state, _ = relay(writes, rates[:, heads:], passed)
    last = rings[-1].last
    lent_state, last_own, backs, last, crossed = gate(
        lent_state, mixed_own[-1], backs, last, crossed
    )
    rings[-1].last = last

    late = len(rings)
    for parts, returned in zip(far_near, backs):
        stage = [jnp.where(is_end, e, m) for e, m in zip(returned, parts)]
        rings.append(ChipRing(tie(jnp.concatenate(stage, axis=0), last)))

    crossed.append(cross(last_own))
    for h, unit in enumerate(lent_units):
        if h == len(lent_units) - 1:
            unit = unit.tied(crossed[kv_heads - 1][1:])
        crossed.append(cross(unit.attend(lent_state[h * groups : (h + 1) * groups])))

    def join(arrays):
        both = jnp.concatenate(arrays, axis=1)
        return both[:, : heads * HEAD], both[:, heads * HEAD :]

    home = join([c[0] for c in crossed])
    returned = join([c[1] for c in crossed])
    near_mixed = [join([c[2][at] for c in crossed]) for at in range(len(turns))]
    far_mixed = [join([c[3][at] for c in crossed]) for at in range(len(turns))]
    ends = [returned[1], returned[0]] + [m[0] for m in far_mixed] + [m[1] for m in far_mixed]
    mids = [home[0]] + [m[0] for m in near_mixed] + [home[1]] + [m[1] for m in near_mixed]
    mixed = [jnp.where(is_end, e, m) for e, m in zip(ends, mids)]
    early = jnp.concatenate(mixed[: -len(turns)], axis=1)
    mixed = jnp.concatenate(mixed[-len(turns) :], axis=1)

    held = [(ring.right, ring.left) for ring in rings[late:]]
    early, mixed, held = gate(early, mixed, held)
    for ring, (right, left) in zip(rings[late:], held):
        ring.right, ring.left = right, left
        ring.close()
    other_early, other = swap_cores(early), swap_cores(mixed)
    base = pad_rows(tokens)
    begun = output_product(early, other_early, base, w_out, ids, [r.pieces() for r in rings[:late]])
    for ring in rings[late:]:
        ring.last = tie(ring.last, begun)
    far_pieces = [ring.pieces() for ring in rings[late:]]
    result, other = output_product(mixed, other, base, w_out, ids, far_pieces, begun)
    other = swap_cores(other)
    start = (1 - core) * half
    base = lax.dynamic_slice_in_dim(base, start, half, 1)
    other = (base.astype(jnp.float32) + other.astype(jnp.float32)).astype(jnp.bfloat16)
    result = lax.dynamic_update_slice_in_dim(result, other, start, 1)
    return result[: tokens.shape[0]]


def solution(mesh):
    return jax.shard_map(
        per_device,
        mesh=mesh,
        in_specs=(
            P(("seg", "tensor"), None),
            P("tensor", None),
            P(),
            P(None, "tensor"),
            P(None, "tensor"),
            P(None, "tensor"),
            P("tensor", None),
            P("seg", "tensor"),
        ),
        out_specs=P(("seg", "tensor"), None),
        check_vma=False,
    )
```
